256 devices in a mesh: sx: 32 (over y_lo, z, core), sy: 4 (over x), ch: 2 (over y_hi).
Axes of the slice: x: 4, y: 4 (y_hi: 2, y_lo: 2; y = y_hi * 2 + y_lo), z: 8, core: 2. Of those that a mesh axis runs over, the one named last changes fastest.
Arguments:
- volume: bfloat16 [4, 256, 16, 512], P(None, ('sx', 'ch'), 'sy'), may hold values from -6 to 6
- w_first: bfloat16 [32, 108], replicated, may hold values from -0.625 to 0.625
- w_second: bfloat16 [64, 864], replicated, may hold values from -0.21875 to 0.21875
- w_third: bfloat16 [128, 1728], replicated, may hold values from -0.15625 to 0.15625
- w_deep: bfloat16 [256, 3456], P(('sy', 'ch')), may hold values from -0.109375 to 0.109375
- grad_out: bfloat16 [256, 64, 4, 128], P(('sy', 'ch'), 'sx'), may hold values from -6 to 6
Outputs:
- activ: bfloat16 [256, 64, 4, 128], P(('sy', 'ch'), 'sx')
- grad_w1: float32 [32, 108], replicated
- grad_w2: float32 [64, 864], replicated
- grad_w3: float32 [128, 1728], replicated
- grad_w4: float32 [256, 3456], P(('sy', 'ch'))
The draws below stay inside these ranges and needn't reach their ends.
All inputs are finite; a program needn't handle non-finite values.
Results may differ from the reference program's by a relative error of at most 0.03.
Values may be sent and summed in bfloat16 or wider, within the bound.
A program may use at most 128 MiB of HBM per device.

```python
import math
import jax
import jax.numpy as jnp
from jax import lax

CIN = 4
C1 = 32
C2 = 64
C3 = 128
C4 = 256
WID = 512
DEPTH = 256
HEIGHT = 16
CELLS4 = 32768


def level_of(rng, dims, split, low, largest):
    level, own = 1.0, jax.random.fold_in(rng, 6)
    for dim, shards_of in split:
        draws = jnp.exp(jax.random.uniform(jax.random.fold_in(own, dim), (shards_of,), jnp.float32, low / len(split), largest / len(split)))
        level = level * jnp.repeat(draws, dims[dim] // shards_of).reshape([-1 if axis == dim else 1 for axis in range(len(dims))])
    return level


def scatter_about(key, extent, spread, limit, pieces=(), dtype=jnp.bfloat16):
    drawn = spread * jax.random.normal(key, extent, jnp.float32)
    if pieces:
        drawn = drawn * level_of(key, extent, pieces, -0.22, 0.18)
    return jnp.clip(drawn, -limit, limit).astype(dtype)


def setup_inputs(seed: int = 0) -> dict:
    streams_of = jax.random.split(jax.random.key(seed), 7)
    return {
        "volume": scatter_about(streams_of[0], (CIN, DEPTH, HEIGHT, WID), 1.0, 6.0, ((1, 64), (2, 4))),
        "w_first": scatter_about(streams_of[1], (C1, 27 * CIN), (27 * CIN) ** -0.5, 0.625),
        "w_second": scatter_about(streams_of[2], (C2, 27 * C1), (27 * C1) ** -0.5, 0.21875),
        "w_third": scatter_about(streams_of[3], (C3, 27 * C2), (27 * C2) ** -0.5, 0.15625),
        "w_deep": scatter_about(streams_of[4], (C4, 27 * C3), (27 * C3) ** -0.5, 0.109375, ((0, 8),)),
        "grad_out": scatter_about(streams_of[5], (C4, DEPTH // 4, HEIGHT // 4, WID // 4), 1.0, 6.0, ((0, 8), (1, 32))),
    }


def smooth_unit(values):
    return 0.3 * values + 0.7 * values * jax.nn.sigmoid(values)

def smooth_slope(values):
    sigma = jax.nn.sigmoid(values)
    return 0.3 + 0.7 * (sigma + values * sigma * (1.0 - sigma))

def to_kernel(weight, channels):
    filters = weight.shape[0]
    shaped = weight.astype(jnp.float32).reshape(filters, 3, 3, 3, channels)
    return jnp.transpose(shaped, (0, 4, 1, 2, 3))

def convolve(field, kernel, stride):
    if stride == 2:
        padding = [(1, 0), (1, 0), (1, 0)]
    else:
        padding = [(1, 1), (1, 1), (1, 1)]
    result = lax.conv_general_dilated(field[None], kernel, (stride, stride, stride), padding, dimension_numbers=('NCDHW', 'OIDHW', 'NCDHW'), precision=lax.Precision.HIGHEST)
    return result[0]

def backward(field, weight, cotangent, stride, channels):
    kernel = to_kernel(weight, channels)

    def apply_conv(inner_field, inner_kernel):
        return convolve(inner_field, inner_kernel, stride)
    unused, pullback = jax.vjp(apply_conv, field.astype(jnp.float32), kernel)
    field_grad, kernel_grad = pullback(cotangent.astype(jnp.float32))
    weight_grad = jnp.transpose(kernel_grad, (0, 2, 3, 4, 1)).reshape(weight.shape)
    return (field_grad, weight_grad)

def reference(volume, w_first, w_second, w_third, w_deep, grad_out):
    pre_one = convolve(volume.astype(jnp.float32), to_kernel(w_first, CIN), 2)
    act_one = smooth_unit(pre_one).astype(jnp.bfloat16)
    pre_two = convolve(act_one.astype(jnp.float32), to_kernel(w_second, C1), 2)
    act_two = smooth_unit(pre_two).astype(jnp.bfloat16)
    pre_three = convolve(act_two.astype(jnp.float32), to_kernel(w_third, C2), 1)
    act_three = smooth_unit(pre_three).astype(jnp.bfloat16)
    pre_deep = convolve(act_three.astype(jnp.float32), to_kernel(w_deep, C3), 1)
    activ = smooth_unit(pre_deep).astype(jnp.bfloat16)
    scale = 1.0 / math.sqrt(CELLS4)
    grad_deep = (grad_out.astype(jnp.float32) * smooth_slope(pre_deep) * scale).astype(jnp.bfloat16)
    back_three, grad_w4 = backward(act_three, w_deep, grad_deep, 1, C3)
    grad_three = (back_three * smooth_slope(pre_three)).astype(jnp.bfloat16)
    back_two, grad_w3 = backward(act_two, w_third, grad_three, 1, C2)
    grad_two = (back_two * smooth_slope(pre_two)).astype(jnp.bfloat16)
    back_one, grad_w2 = backward(act_one, w_second, grad_two, 2, C1)
    grad_one = (back_one * smooth_slope(pre_one)).astype(jnp.bfloat16)
    unused_grad, grad_w1 = backward(volume, w_first, grad_one, 2, CIN)
    return (activ, grad_w1, grad_w2, grad_w3, grad_w4)
```

```python
import functools
import jax
import jax.numpy as jnp
from jax import lax
from jax.experimental import pallas as pl
from jax.experimental.pallas import tpu as pltpu
from jax.sharding import PartitionSpec as P

MESH = pl.DeviceIdType.MESH
BF = jnp.bfloat16
F32 = jnp.float32
N3, N2, N4 = 27, 30, 27


def plane_place(rank, z):
    sy = lax.rem(rank, 4)
    ch = lax.rem(lax.div(rank, 4), 2)
    core = lax.rem(lax.div(rank, 8), 2)
    low = lax.div(rank, 16)
    return (low * 16 + z * 2 + core, sy, ch)


def await_bytes(ref, sem):
    pltpu.make_async_copy(ref, ref, sem).wait()


def sum_kernel(
    a3, a2, a4, o3, o2, o4,
    in3, in2, in4, mid3, mid2, part3, part2, all3, all2, all4,
    send, recv,
):
    sx, sy, ch = lax.axis_index("sx"), lax.axis_index("sy"), lax.axis_index("ch")
    core = lax.rem(sx, 2)
    z = lax.rem(lax.div(sx, 2), 8)
    low = lax.div(sx, 16)
    rank = low * 16 + core * 8 + ch * 4 + sy

    def plane(k):
        other = lax.rem(rank + k, 32)
        return other, plane_place(other, z)

    def column(k):
        other = lax.rem(z + k, 8)
        return other, (low * 16 + other * 2 + core, sy, ch)

    def depth(k):
        other = lax.rem(sx + k, 32)
        return other, (other, sy, ch)

    barrier = pltpu.get_barrier_semaphore()

    def greet(count, where):
        def step(k, carry):
            pl.semaphore_signal(barrier, inc=1, device_id=where(k)[1], device_id_type=MESH)
            return carry
        lax.fori_loop(1, count, step, 0)

    greet(32, plane)
    greet(8, column)
    greet(32, depth)
    pl.semaphore_wait(barrier, 31 + 7 + 31)

    def scatter(count, where, shards, src, dst, mine, slot):
        def step(k, carry):
            other, place = where(k)

            @pl.when(other < shards)
            def _():
                pltpu.make_async_remote_copy(
                    src_ref=src.at[other], dst_ref=dst.at[mine],
                    send_sem=send.at[slot], recv_sem=recv.at[slot],
                    device_id=place, device_id_type=MESH,
                ).start()
            return carry
        lax.fori_loop(1, count, step, 0)

    def spread(count, where, src, dst, slot):
        def step(k, carry):
            other, place = where(k)
            pltpu.make_async_remote_copy(
                src_ref=src, dst_ref=dst,
                send_sem=send.at[slot], recv_sem=recv.at[slot],
                device_id=place, device_id_type=MESH,
            ).start()
            return carry
        lax.fori_loop(1, count, step, 0)

    def total(ref, count):
        def step(i, acc):
            return acc + ref[i].astype(F32)
        return lax.fori_loop(0, count, step, jnp.zeros(ref.shape[1:], F32))

    scatter(32, plane, N2, a2, in2, rank, 0)
    scatter(32, plane, N3, a3, in3, rank, 1)
    scatter(32, depth, N4, a4, in4, sx, 2)

    @pl.when(rank < N2)
    def _():
        in2[rank] = a2[rank]
        await_bytes(in2.at[pl.ds(0, 31)], recv.at[0])
        part2[...] = total(in2, 32).astype(BF)
        mid2[z] = part2[...]
        spread(8, column, part2, mid2.at[z], 3)

    @pl.when(rank < N3)
    def _():
        in3[rank] = a3[rank]
        await_bytes(in3.at[pl.ds(0, 31)], recv.at[1])
        part3[...] = total(in3, 32).astype(BF)
        mid3[z] = part3[...]
        spread(8, column, part3, mid3.at[z], 4)

    @pl.when(sx < N4)
    def _():
        in4[sx] = a4[sx]
        await_bytes(in4.at[pl.ds(0, 31)], recv.at[2])
        all4[sx] = total(in4, 32).astype(BF)
        spread(32, depth, all4.at[sx], all4.at[sx], 5)

    @pl.when(rank < N2)
    def _():
        await_bytes(mid2.at[pl.ds(0, 7)], recv.at[3])
        all2[rank] = total(mid2, 8).astype(BF)
        spread(32, plane, all2.at[rank], all2.at[rank], 6)

    @pl.when(rank < N3)
    def _():
        await_bytes(mid3.at[pl.ds(0, 7)], recv.at[4])
        all3[rank] = total(mid3, 8).astype(BF)
        spread(32, plane, all3.at[rank], all3.at[rank], 7)

    def finish(me, shards, buf, out, slot):
        @pl.when(me < shards)
        def _():
            await_bytes(buf.at[pl.ds(0, shards - 1)], recv.at[slot])

        @pl.when(me >= shards)
        def _():
            await_bytes(buf.at[pl.ds(0, shards)], recv.at[slot])

        def step(i, carry):
            out[i] = buf[i].astype(F32)
            return carry
        lax.fori_loop(0, shards, step, 0)

    finish(sx, N4, all4, o4, 5)
    finish(rank, N2, all2, o2, 6)
    finish(rank, N3, all3, o3, 7)

    def sent(me, shards, src, slot):
        @pl.when(me < shards)
        def _():
            await_bytes(src.at[pl.ds(0, shards - 1)], send.at[slot])

        @pl.when(me >= shards)
        def _():
            await_bytes(src.at[pl.ds(0, shards)], send.at[slot])

    sent(rank, N2, a2, 0)
    sent(rank, N3, a3, 1)
    sent(sx, N4, a4, 2)

    @pl.when(rank < N2)
    def _():
        await_bytes(mid2.at[pl.ds(0, 7)], send.at[3])
        await_bytes(in2.at[pl.ds(0, 31)], send.at[6])

    @pl.when(rank < N3)
    def _():
        await_bytes(mid3.at[pl.ds(0, 7)], send.at[4])
        await_bytes(in3.at[pl.ds(0, 31)], send.at[7])

    @pl.when(sx < N4)
    def _():
        await_bytes(in4.at[pl.ds(0, 31)], send.at[5])


def sum_all(a3, a2, a4):
    vmem = pl.BlockSpec(memory_space=pltpu.VMEM)
    return pl.pallas_call(
        sum_kernel,
        out_shape=(
            jax.ShapeDtypeStruct((N3, 64, 128), F32),
            jax.ShapeDtypeStruct((N2, 16, 128), F32),
            jax.ShapeDtypeStruct((N4, 32, 128), F32),
        ),
        in_specs=[vmem] * 3,
        out_specs=(vmem,) * 3,
        scratch_shapes=[
            pltpu.VMEM((32, 64, 128), BF),
            pltpu.VMEM((32, 16, 128), BF),
            pltpu.VMEM((32, 32, 128), BF),
            pltpu.VMEM((8, 64, 128), BF),
            pltpu.VMEM((8, 16, 128), BF),
            pltpu.VMEM((64, 128), BF),
            pltpu.VMEM((16, 128), BF),
            pltpu.VMEM((N3, 64, 128), BF),
            pltpu.VMEM((N2, 16, 128), BF),
            pltpu.VMEM((N4, 32, 128), BF),
            pltpu.SemaphoreType.DMA((8,)),
            pltpu.SemaphoreType.DMA((8,)),
        ],
        compiler_params=pltpu.CompilerParams(
            collective_id=1, has_side_effects=True, vmem_limit_bytes=32 * 1024 * 1024
        ),
        name="sum_filter_gradients",
    )(a3, a2, a4)


def shifted(value, axis, by):
    length = lax.axis_size(axis)
    pairs = [(i, i + by) for i in range(length) if 0 <= i + by < length]
    return lax.ppermute(value, axis, pairs)


def padded_2(value, sides, width):
    for axis, dim in sides:
        size, length = (lax.axis_size(axis), value.shape[dim])
        up = [(i, (i + 1) % size) for i in range(size - 1)]
        down = [(j, i) for i, j in up]
        last = lax.slice_in_dim(value, length - width, length, axis=dim)
        first = lax.slice_in_dim(value, 0, width, axis=dim)
        before = lax.ppermute(last, axis, up)
        after = lax.ppermute(first, axis, down)
        value = jnp.concatenate([before, value, after], axis=dim)
    return value


def smooth_unit(values):
    return 0.3 * values + 0.7 * values * jax.nn.sigmoid(values)


def smooth_slope(values):
    sigma = jax.nn.sigmoid(values)
    return 0.3 + 0.7 * (sigma + values * sigma * (1.0 - sigma))


def tap_block(padded, depth_tap, extent, stride):
    depth, height, width = extent
    pieces = []
    for row_tap in range(3):
        for col_tap in range(3):
            pieces.append(
                padded[
                    :,
                    depth_tap : depth_tap + stride * (depth - 1) + 1 : stride,
                    row_tap : row_tap + stride * (height - 1) + 1 : stride,
                    col_tap : col_tap + stride * (width - 1) + 1 : stride,
                ]
            )
    stacked = jnp.concatenate(pieces, axis=0)
    return stacked.reshape(stacked.shape[0], depth * height * width)


def conv_apply(padded, weight, extent, stride):
    channels = padded.shape[0]
    summed = None
    for depth_tap in range(3):
        stacked = tap_block(padded, depth_tap, extent, stride)
        columns = weight[:, depth_tap * 9 * channels : (depth_tap + 1) * 9 * channels]
        partial_sum = jnp.dot(columns, stacked, preferred_element_type=jnp.float32)
        summed = partial_sum if summed is None else summed + partial_sum
    return summed.reshape((weight.shape[0],) + tuple(extent))


def weight_grad(padded, cotangent, extent, stride):
    flattened = cotangent.reshape(cotangent.shape[0], -1)
    pieces = []
    for depth_tap in range(3):
        stacked = tap_block(padded, depth_tap, extent, stride)
        pieces.append(
            lax.dot_general(
                flattened, stacked, (((1,), (1,)), ((), ())), preferred_element_type=jnp.float32
            )
        )
    return jnp.concatenate(pieces, axis=1)


def flipped(weight):
    filters = weight.shape[0]
    channels = weight.shape[1] // 27
    shaped = weight.reshape(filters, 27, channels)[:, ::-1, :]
    return jnp.transpose(shaped, (2, 1, 0)).reshape(channels, 27 * filters)


def lower_rims(field):
    plane = shifted(field[:, -1:], ("sx", "ch"), 1)
    field = jnp.concatenate([plane, field], axis=1)
    row_rim = shifted(field[:, :, -1:], "sy", 1)
    field = jnp.concatenate([row_rim, field], axis=2)
    return jnp.pad(field, ((0, 0), (0, 0), (0, 0), (1, 0)))


def upper_rims(field):
    plane = shifted(field, ("sx", "ch"), -1)
    field = jnp.concatenate([field, plane], axis=1)
    row_rim = shifted(field, "sy", -1)
    field = jnp.concatenate([field, row_rim], axis=2)
    return jnp.pad(field, ((0, 0), (0, 0), (0, 0), (0, 1)))


def margins(field):
    padded = padded_2(field, ((("sx", "ch"), 1), ("sy", 2)), 1)
    return jnp.pad(padded, ((0, 0), (0, 0), (0, 0), (1, 1)))


def deep_margins(field):
    padded = padded_2(field, (("sx", 1),), 1)
    return jnp.pad(padded, ((0, 0), (0, 0), (1, 1), (1, 1)))


def spread_back(padded, weight, extent):
    depth, height, width = extent
    filters = padded.shape[0]
    channels = weight.shape[1] // 27
    kernel = weight.reshape(weight.shape[0], 27, channels)
    parity_taps = (((1, 0),), ((0, 1), (2, 0)))
    classes = []
    for depth_par in range(2):
        for row_par in range(2):
            for col_par in range(2):
                column_list = []
                weight_list = []
                for depth_tap, depth_off in parity_taps[depth_par]:
                    for row_tap, row_off in parity_taps[row_par]:
                        for col_tap, col_off in parity_taps[col_par]:
                            piece = padded[
                                :,
                                depth_off : depth_off + depth,
                                row_off : row_off + height,
                                col_off : col_off + width,
                            ]
                            column_list.append(piece.reshape(filters, depth * height * width))
                            weight_list.append(kernel[:, 9 * depth_tap + 3 * row_tap + col_tap, :])
                stacked = jnp.concatenate(column_list, axis=0)
                weight_stack = jnp.concatenate(weight_list, axis=0)
                classes.append(
                    lax.dot_general(
                        weight_stack,
                        stacked,
                        (((0,), (0,)), ((), ())),
                        preferred_element_type=jnp.float32,
                    )
                )
    merged = jnp.stack(classes, axis=0).reshape(2, 2, 2, channels, depth, height, width)
    merged = jnp.transpose(merged, (3, 4, 0, 5, 1, 6, 2))
    return merged.reshape(channels, 2 * depth, 2 * height, 2 * width)


def to_deep(pieces, groups_sy, groups_ch):
    count, channels, depth, height, width = pieces.shape
    shaped = pieces.reshape(groups_sy, groups_ch, channels, depth, height, width)
    shaped = jnp.transpose(shaped, (2, 1, 3, 0, 4, 5))
    return shaped.reshape(channels, groups_ch * depth, groups_sy * height, width)


def from_deep(field, groups_sy, groups_ch):
    channels, depth_all, height_all, width = field.shape
    depth = depth_all // groups_ch
    height = height_all // groups_sy
    shaped = field.reshape(channels, groups_ch, depth, groups_sy, height, width)
    shaped = jnp.transpose(shaped, (3, 1, 0, 2, 4, 5))
    return shaped.reshape(groups_sy * groups_ch, channels, depth, height, width)


def per_device(volume, w_first, w_second, w_third, w_deep, grad_out):
    groups_sy = lax.axis_size("sy")
    groups_ch = lax.axis_size("ch")
    depth_in, height_in, width_in = (volume.shape[1], volume.shape[2], volume.shape[3])
    extent_one = (depth_in // 2, height_in // 2, width_in // 2)
    extent_two = (depth_in // 4, height_in // 4, width_in // 4)
    padded_vol = lower_rims(volume)
    pre_one = conv_apply(padded_vol, w_first, extent_one, 2)
    act_one = smooth_unit(pre_one).astype(jnp.bfloat16)
    padded_one = lower_rims(act_one)
    pre_two = conv_apply(padded_one, w_second, extent_two, 2)
    act_two = smooth_unit(pre_two).astype(jnp.bfloat16)
    padded_two = margins(act_two)
    pre_three = conv_apply(padded_two, w_third, extent_two, 1)
    act_three = smooth_unit(pre_three).astype(jnp.bfloat16)
    gathered = lax.all_gather(act_three[None], ("sy", "ch"), axis=0, tiled=True)
    deep_input = to_deep(gathered, groups_sy, groups_ch)
    extent_deep = deep_input.shape[1:]
    padded_deep = deep_margins(deep_input)
    pre_deep = conv_apply(padded_deep, w_deep, extent_deep, 1)
    activ = smooth_unit(pre_deep).astype(jnp.bfloat16)
    cells_all = extent_deep[0] * lax.axis_size("sx") * extent_deep[1] * extent_deep[2]
    scale = 1.0 / float(cells_all) ** 0.5
    grad_deep = (grad_out.astype(jnp.float32) * smooth_slope(pre_deep) * scale).astype(jnp.bfloat16)
    local_w4 = weight_grad(padded_deep, grad_deep, extent_deep, 1)
    padded_grad = padded_2(grad_deep, (("sx", 1),), 1)
    padded_grad = jnp.pad(padded_grad, ((0, 0), (0, 0), (1, 1), (1, 1)))
    partial_back = conv_apply(padded_grad, flipped(w_deep), extent_deep, 1)
    pieces = from_deep(partial_back, groups_sy, groups_ch)
    back_three = lax.psum_scatter(
        pieces.astype(jnp.bfloat16), ("sy", "ch"), scatter_dimension=0, tiled=True
    ).astype(jnp.float32)[0]
    grad_three = (back_three * smooth_slope(pre_three)).astype(jnp.bfloat16)
    local_w3 = weight_grad(padded_two, grad_three, extent_two, 1)
    padded_three = margins(grad_three)
    back_two = conv_apply(padded_three, flipped(w_third), extent_two, 1)
    grad_two = (back_two * smooth_slope(pre_two)).astype(jnp.bfloat16)
    local_w2 = weight_grad(padded_one, grad_two, extent_two, 2)
    padded_back = upper_rims(grad_two)
    back_one = spread_back(padded_back, w_second, extent_two)
    grad_one = (back_one * smooth_slope(pre_one)).astype(jnp.bfloat16)
    local_w1 = weight_grad(padded_vol, grad_one, extent_one, 2)
    a3 = jnp.transpose(local_w3.astype(BF).reshape(128, 27, 64), (1, 2, 0))
    wide2 = jnp.pad(local_w2.astype(BF), ((0, 0), (0, 32))).reshape(4, 16, 7, 128)
    wide1 = jnp.pad(local_w1.astype(BF), ((0, 0), (0, 20))).reshape(2, 16, 128)
    a2 = jnp.concatenate([jnp.transpose(wide2, (2, 0, 1, 3)).reshape(28, 16, 128), wide1], axis=0)
    a4 = jnp.transpose(local_w4.astype(BF).reshape(32, 27, 128), (1, 0, 2))
    s3, s2, s4 = sum_all(a3, a2, a4)
    grad_w3 = jnp.transpose(s3, (2, 0, 1)).reshape(128, 1728)
    grad_w2 = jnp.transpose(s2[:28].reshape(7, 4, 16, 128), (1, 2, 0, 3)).reshape(64, 896)[:, :864]
    grad_w1 = s2[28:].reshape(32, 128)[:, :108]
    grad_w4 = jnp.transpose(s4, (1, 0, 2)).reshape(32, 3456)
    return (activ, grad_w1, grad_w2, grad_w3, grad_w4)


def solution(mesh):
    placed = (
        P(None, ("sx", "ch"), "sy", None),
        P(),
        P(),
        P(),
        P(("sy", "ch"), None),
        P(("sy", "ch"), "sx", None, None),
    )
    return jax.shard_map(
        per_device,
        mesh=mesh,
        in_specs=placed,
        out_specs=(P(("sy", "ch"), "sx", None, None), P(), P(), P(), P(("sy", "ch"), None)),
        check_vma=False,
    )
```

```python
import numpy as np
import jax
import jax.numpy as jnp
from jax import lax
from jax.experimental import pallas as pl
from jax.experimental.pallas import tpu as pltpu
from jax.sharding import PartitionSpec as P

MESH = pl.DeviceIdType.MESH
BF = jnp.bfloat16
F32 = jnp.float32
N3, N2, N4 = 27, 30, 27


def row_choice():
    pick = np.zeros((224, 256), np.float32)
    for d in range(7):
        for h in range(7):
            block = (0 if d >= 3 else 1) + (0 if h >= 3 else 2)
            for c in range(4):
                source = block * 64 + c * 16 + ((d + 1) % 4) * 4 + (h + 1) % 4
                pick[d * 32 + h * 4 + c, source] = 1.0
    return pick


def band_choice():
    pick = np.zeros((3, 128, 288), np.float32)
    for j in range(3):
        for kd in range(3):
            for kh in range(3):
                for kw in range(3):
                    for c in range(4):
                        pick[j, (9 * kd + 3 * kh + kw) * 4 + c, kw * 96 + kd * 32 + (2 * j + kh) * 4 + c] = 1.0
    return pick


def smooth_unit(values):
    return 0.3 * values + 0.7 * values * jax.nn.sigmoid(values)


def smooth_slope(values):
    sigma = jax.nn.sigmoid(values)
    return 0.3 + 0.7 * (sigma + values * sigma * (1.0 - sigma))


def mm(a, b):
    return jnp.dot(a, b, preferred_element_type=F32)


def mm_nt(a, b):
    return lax.dot_general(a, b, (((1,), (1,)), ((), ())), preferred_element_type=F32)


def lane_of(shape):
    return lax.broadcasted_iota(jnp.int32, shape, len(shape) - 1)


def from_left(x):
    return jnp.where(lane_of(x.shape) == 0, 0.0, pltpu.roll(x, 1, 1))


def from_right(x):
    return jnp.where(lane_of(x.shape) == 127, 0.0, pltpu.roll(x, 127, 1))


def await_bytes(ref, sem):
    pltpu.make_async_copy(ref, ref, sem).wait()


def whole_kernel(
    vol, w1, w2, w3, w4, gout, rows_pick, band,
    activ, o1, o2, o3, o4,
    perm, w1band, wbk_t, wbk, wb4_t, wb4, w3b,
    vin, vst, p1, a1, gath, x2s, s2own, s2buf, p3, x3s,
    g4send, g4halo, g4s, rs_send, rs_recv, g3own, g3buf, g3s, g2st,
    a3, a2, a4, in3, in2, in4, mid3, mid2, part3, part2, all3, all2, all4,
    send, recv, scale,
):
    sx, sy, ch = lax.axis_index("sx"), lax.axis_index("sy"), lax.axis_index("ch")
    core = lax.rem(sx, 2)
    z = lax.rem(lax.div(sx, 2), 8)
    low = lax.div(sx, 16)
    rank = low * 16 + core * 8 + ch * 4 + sy
    g = sx * 2 + ch
    cell = ch * 4 + sy

    def block_place(depth_block, row_block):
        d = lax.rem(depth_block + 64, 64)
        return (lax.div(d, 2), lax.rem(row_block + 4, 4), lax.rem(d, 2))

    def near(k):
        other = lax.rem(cell + 8 + k, 24)
        group = lax.div(other, 8) - 1
        return group, (lax.rem(sx + group + 32, 32), lax.rem(other, 4), lax.rem(lax.div(other, 4), 2))

    def plane(k):
        other = lax.rem(rank + k, 32)
        place = (
            lax.div(other, 16) * 16 + z * 2 + lax.rem(lax.div(other, 8), 2),
            lax.rem(other, 4),
            lax.rem(lax.div(other, 4), 2),
        )
        return other, place

    def column(k):
        other = lax.rem(z + k, 8)
        return other, (low * 16 + other * 2 + core, sy, ch)

    def depth(k):
        other = lax.rem(sx + k, 32)
        return other, (other, sy, ch)

    def loop(count, step, start=1):
        def body(k, carry):
            step(k)
            return carry
        lax.fori_loop(start, count, body, 0)

    def push(src, dst, slot, place):
        pltpu.make_async_remote_copy(
            src_ref=src, dst_ref=dst, send_sem=send.at[slot], recv_sem=recv.at[slot],
            device_id=place, device_id_type=MESH,
        ).start()

    barrier = pltpu.get_barrier_semaphore()

    def greet(count, where):
        def step(k):
            pl.semaphore_signal(barrier, inc=1, device_id=where(k)[1], device_id_type=MESH)
        loop(count, step)

    greet(24, near)
    greet(32, plane)
    greet(8, column)
    greet(32, depth)

    for p in range(4):
        r = lax.broadcasted_iota(jnp.int32, (512, 128), 0)
        perm[:, p * 128 : (p + 1) * 128] = jnp.where(r == 4 * lane_of((512, 128)) + p, 1.0, 0.0).astype(BF)
    for j in range(3):
        w1band[j * 32 : (j + 1) * 32, :] = mm(w1[...], band[j, :108, :]).astype(BF)
    pl.semaphore_wait(barrier, 23 + 31 + 7 + 31)

    push(vol, vin.at[0], 0, block_place(g + 1, sy))
    push(vol, vin.at[1], 0, block_place(g, sy + 1))
    push(vol, vin.at[2], 0, block_place(g + 1, sy + 1))

    zero = jnp.zeros((96, 128), BF)
    for d in range(6):
        for h in (0, 5):
            at = (d * 6 + h) * 128
            for r in range(2):
                x2s[r * 96 : (r + 1) * 96, at : at + 128] = zero
            if d < 4:
                g4s[:, at : at + 128] = zero
                for r in range(4):
                    x3s[r * 96 : (r + 1) * 96, at : at + 128] = zero
    for t in range(27):
        wb4_t[t * 32 : (t + 1) * 32, :] = w4[:, (26 - t) * 128 : (27 - t) * 128]
    wb4_t[864:896, :] = jnp.zeros((32, 128), BF)
    for k in range(7):
        wb4[:, k * 128 : (k + 1) * 128] = wb4_t[k * 128 : (k + 1) * 128, :].astype(F32).T.astype(BF)
    for k in range(14):
        if k < 13:
            turned = w3[:, k * 128 : (k + 1) * 128].astype(F32).T.astype(BF)
        else:
            turned = w3[:, 1664:1728].astype(F32).T.astype(BF)
        w3b[:, (26 - 2 * k) * 128 : (27 - 2 * k) * 128] = turned[:64]
        if k < 13:
            w3b[:, (25 - 2 * k) * 128 : (26 - 2 * k) * 128] = turned[64:]
    wbk_t[...] = jnp.zeros((512, 256), BF)
    taps = {(0, 0): 1, (1, 0): 2, (1, 1): 0}
    for (pa, a), kd in taps.items():
        for (pb, b), kh in taps.items():
            for (pe, s), kw in taps.items():
                r = (a * 4 + b * 2 + s) * 64
                c = (pa * 4 + pe * 2 + pb) * 32
                t = (9 * kd + 3 * kh + kw) * 32
                wbk_t[r : r + 64, c : c + 32] = w2[:, t : t + 32]
    for r in range(4):
        for c in range(2):
            block = wbk_t[r * 128 : (r + 1) * 128, c * 128 : (c + 1) * 128]
            wbk[c * 128 : (c + 1) * 128, r * 128 : (r + 1) * 128] = block.astype(F32).T.astype(BF)

    await_bytes(vin, recv.at[0])
    none = jnp.zeros((64, 512), BF)
    blocks = jnp.concatenate(
        [
            vol[...],
            jnp.where(g > 0, vin[0], none),
            jnp.where(sy > 0, vin[1], none),
            jnp.where((g > 0) & (sy > 0), vin[2], none),
        ],
        axis=0,
    )
    ordered = mm(mm(rows_pick[...], blocks).astype(BF), perm[...])
    phases = [ordered[:, p * 128 : (p + 1) * 128] for p in range(4)]
    before = from_left(phases[3]).astype(BF)
    phases = [x.astype(BF) for x in phases]
    for q, used in enumerate(((before, phases[0], phases[1]), (phases[1], phases[2], phases[3]))):
        for kw in range(3):
            for i in range(3):
                at = (2 * i + q) * 128
                vst[kw * 96 : (kw + 1) * 96, at : at + 128] = used[kw][64 * i : 64 * i + 96]
    pre_one = mm(w1band[...], vst[...])
    p1[...] = pre_one[32:, 256:]
    act_one = smooth_unit(pre_one)
    for i in range(3):
        even = act_one[:, (2 * i) * 128 : (2 * i + 1) * 128]
        odd = act_one[:, (2 * i + 1) * 128 : (2 * i + 2) * 128]
        three = (from_left(odd).astype(BF), even.astype(BF), odd.astype(BF))
        for j in range(3):
            for kw in range(3):
                r = (3 * i + j) * 96 + kw * 32
                a1[r : r + 32, :] = three[kw][j * 32 : (j + 1) * 32]
    pre_two = mm(w2[...], a1[...])
    act_two = smooth_unit(pre_two).astype(BF)
    own = (ch + 2) * 4 + sy
    gath[own] = act_two

    def send_act(k):
        group, place = near(k)
        push(gath.at[own], gath.at[own - 8 * group], 1, place)
    loop(24, send_act)
    slope_two = smooth_slope(pre_two)
    s2own[...] = slope_two
    s2buf[0] = slope_two
    push(s2own, s2buf.at[1], 2, block_place(g, sy - 1))
    push(s2own, s2buf.at[2], 2, block_place(g - 1, sy))
    push(s2own, s2buf.at[3], 2, block_place(g - 1, sy - 1))
    await_bytes(gath.at[pl.ds(0, 23)], recv.at[1])

    def spread_three(ref, rows, at, x, keep):
        if keep is not None:
            x = jnp.where(keep, x, 0.0)
        ref[0:rows, pl.ds(at, 128)] = from_left(x).astype(BF)
        ref[rows : 2 * rows, pl.ds(at, 128)] = x.astype(BF)
        ref[2 * rows : 3 * rows, pl.ds(at, 128)] = from_right(x).astype(BF)

    for d in range(6):
        keep = sx > 0 if d < 2 else (sx < 31 if d > 3 else None)
        for h in range(4):
            spread_three(x2s, 64, (d * 6 + h + 1) * 128, gath[d * 4 + h].astype(F32), keep)

    def taps_of(ref, p):
        return jnp.concatenate(
            [ref[:, ((p + kd) * 6 + kh) * 128 : ((p + kd) * 6 + kh + 4) * 128] for kd in range(3) for kh in range(3)],
            axis=0,
        )

    for p in range(4):
        pre = mm(w3[...], taps_of(x2s, p))
        act = smooth_unit(pre)
        keep = sx > 0 if p == 0 else (sx < 31 if p == 3 else None)
        for h in range(4):
            piece = slice(h * 128, (h + 1) * 128)
            if p in (1, 2):
                p3[(p - 1) * 4 + h] = pre[:, piece]
            spread_three(x3s, 128, (p * 6 + h + 1) * 128, act[:, piece].astype(BF).astype(F32), keep)

    grads = []
    for p in range(2):
        pre = mm(w4[...], taps_of(x3s, p))
        here = slice(p * 512, (p + 1) * 512)
        activ[:, here] = smooth_unit(pre).astype(BF)
        grad = (gout[:, here].astype(F32) * smooth_slope(pre) * scale).astype(BF)
        grads.append(grad)
        g4send[p] = grad
    push(g4send.at[0], g4halo.at[1], 3, (lax.rem(sx + 31, 32), sy, ch))
    push(g4send.at[1], g4halo.at[0], 3, (lax.rem(sx + 1, 32), sy, ch))
    for kd in range(3):
        for kh in range(3):
            part = None
            for p in range(2):
                at = ((p + kd) * 6 + kh) * 128
                more = mm_nt(grads[p], x3s[:, at : at + 512])
                part = more if part is None else part + more
            for kw in range(3):
                a4[9 * kd + 3 * kh + kw] = part[:, kw * 128 : (kw + 1) * 128].astype(BF)
    for p in range(2):
        for h in range(4):
            x = grads[p][:, h * 128 : (h + 1) * 128].astype(F32)
            spread_three(g4s, 32, ((p + 1) * 6 + h + 1) * 128, x, None)
    await_bytes(g4halo, recv.at[3])
    for e, p, keep in ((0, 0, sx > 0), (1, 3, sx < 31)):
        for h in range(4):
            x = g4halo[e, :, h * 128 : (h + 1) * 128].astype(F32)
            spread_three(g4s, 32, (p * 6 + h + 1) * 128, x, keep)
    for p in range(2):
        back = mm(wb4[:, :864], taps_of(g4s, p)).astype(BF)
        for h in range(4):
            rs_send[p * 4 + h] = back[:, h * 128 : (h + 1) * 128]

    def send_back(k):
        other = lax.rem(cell + k, 8)
        push(rs_send.at[other], rs_recv.at[cell], 4, (sx, lax.rem(other, 4), lax.div(other, 4)))
    loop(8, send_back)

    def scatter(count, where, shards, src, dst, mine, slot):
        def step(k):
            other, place = where(k)

            @pl.when(other < shards)
            def _():
                push(src.at[other], dst.at[mine], slot, place)
        loop(count, step)

    def spread(count, where, src, dst, slot):
        loop(count, lambda k: push(src, dst, slot, where(k)[1]))

    def total(ref):
        return jnp.sum(ref[...].astype(F32), axis=0)

    scatter(32, depth, N4, a4, in4, sx, 8)
    rs_recv[cell] = rs_send[cell]
    await_bytes(rs_recv.at[pl.ds(0, 7)], recv.at[4])
    grad_three = (total(rs_recv) * smooth_slope(p3[cell])).astype(BF)
    g3own[...] = grad_three
    g3buf[5] = grad_three

    def send_three(k):
        slot = lax.rem(5 + k, 16)
        up = lax.div(slot, 4) - 1
        side = lax.rem(slot, 4) - 1
        push(g3own, g3buf.at[slot], 5, block_place(g - up, sy - side))
    loop(16, send_three)

    for kd in range(3):
        for kh in range(3):
            at = pl.multiple_of(((ch + 1 + kd) * 6 + sy + kh) * 128, 128)
            part = mm_nt(x2s[:, pl.ds(at, 128)], grad_three).astype(BF)
            for kw in range(3):
                a3[9 * kd + 3 * kh + kw] = part[kw * 64 : (kw + 1) * 64]
    scatter(32, plane, N3, a3, in3, rank, 9)

    @pl.when(sx < N4)
    def _():
        in4[sx] = a4[sx]
        await_bytes(in4.at[pl.ds(0, 31)], recv.at[8])
        all4[sx] = total(in4).astype(BF)
        spread(32, depth, all4.at[sx], all4.at[sx], 10)

    await_bytes(g3buf.at[pl.ds(0, 15)], recv.at[5])
    for d in range(4):
        for h in range(4):
            keep = (g - 1 + d >= 0) & (g - 1 + d < 64) & (sy - 1 + h >= 0) & (sy - 1 + h < 4)
            spread_three(g3s, 128, (d * 4 + h) * 128, g3buf[d * 4 + h].astype(F32), keep)
    await_bytes(s2buf.at[pl.ds(0, 3)], recv.at[2])
    for a in range(2):
        around = jnp.concatenate(
            [g3s[:, ((a + kd) * 4 + kh) * 128 : ((a + kd) * 4 + kh + 2) * 128] for kd in range(3) for kh in range(3)],
            axis=0,
        )
        back = mm(w3b[...], around)
        for b in range(2):
            x = back[:, b * 128 : (b + 1) * 128] * s2buf[a * 2 + b]
            if a or b:
                keep = (g + a < 64) & (sy + b < 4)
                x = jnp.where(keep, x, 0.0)
            x = x.astype(BF)
            r = (a * 2 + b) * 128
            g2st[r : r + 64, :] = x
            g2st[r + 64 : r + 128, :] = from_right(x.astype(F32)).astype(BF)
    back_one = mm(wbk[...], g2st[...])
    slope_one = smooth_slope(p1[...])
    grad_one = jnp.concatenate(
        [back_one[k * 64 : (k + 1) * 64] * slope_one[:, k * 128 : (k + 1) * 128] for k in range(4)], axis=1
    ).astype(BF)
    banded = mm_nt(grad_one, vst[:, 256:])
    high = banded.astype(BF)
    rest = (banded - high.astype(F32)).astype(BF)
    local_one = jnp.zeros((32, 128), F32)
    for b in range(2):
        local_one += mm_nt(high[b * 32 : (b + 1) * 32], band[b + 1])
        local_one += mm_nt(rest[b * 32 : (b + 1) * 32], band[b + 1])
    local_one = local_one.astype(BF)
    a2[28] = local_one[:16]
    a2[29] = local_one[16:]
    grad_two = g2st[0:64, :]
    for k in range(7):
        size = 128 if k < 6 else 96
        part = mm_nt(grad_two, a1[k * 128 : k * 128 + size, :]).astype(BF)
        if k == 6:
            part = jnp.concatenate([part, jnp.zeros((64, 32), BF)], axis=1)
        for r in range(4):
            a2[k * 4 + r] = part[r * 16 : (r + 1) * 16]
    scatter(32, plane, N2, a2, in2, rank, 11)

    @pl.when(rank < N3)
    def _():
        in3[rank] = a3[rank]
        await_bytes(in3.at[pl.ds(0, 31)], recv.at[9])
        part3[...] = total(in3).astype(BF)
        mid3[z] = part3[...]
        spread(8, column, part3, mid3.at[z], 12)

    @pl.when(rank < N2)
    def _():
        in2[rank] = a2[rank]
        await_bytes(in2.at[pl.ds(0, 31)], recv.at[11])
        part2[...] = total(in2).astype(BF)
        mid2[z] = part2[...]
        spread(8, column, part2, mid2.at[z], 13)

    @pl.when(rank < N3)
    def _():
        await_bytes(mid3.at[pl.ds(0, 7)], recv.at[12])
        all3[rank] = total(mid3).astype(BF)
        spread(32, plane, all3.at[rank], all3.at[rank], 14)

    @pl.when(rank < N2)
    def _():
        await_bytes(mid2.at[pl.ds(0, 7)], recv.at[13])
        all2[rank] = total(mid2).astype(BF)
        spread(32, plane, all2.at[rank], all2.at[rank], 15)

    def arrived(me, shards, buf, slot):
        @pl.when(me < shards)
        def _():
            await_bytes(buf.at[pl.ds(0, shards - 1)], recv.at[slot])

        @pl.when(me >= shards)
        def _():
            await_bytes(buf.at[pl.ds(0, shards)], recv.at[slot])

    arrived(sx, N4, all4, 10)
    for t in range(27):
        o4[:, t * 128 : (t + 1) * 128] = all4[t].astype(F32)
    arrived(rank, N3, all3, 14)
    for k in range(14):
        if k < 13:
            pair = jnp.concatenate([all3[2 * k], all3[2 * k + 1]], axis=0)
            o3[:, k * 128 : (k + 1) * 128] = pair.astype(F32).T
        else:
            o3[:, 1664:1728] = all3[26].astype(F32).T
    arrived(rank, N2, all2, 15)
    for k in range(7):
        size = 128 if k < 6 else 96
        for r in range(4):
            o2[r * 16 : (r + 1) * 16, k * 128 : k * 128 + size] = all2[k * 4 + r].astype(F32)[:, :size]
    o1[0:16, :] = all2[28].astype(F32)[:, :108]
    o1[16:32, :] = all2[29].astype(F32)[:, :108]

    await_bytes(vin, send.at[0])
    await_bytes(gath.at[pl.ds(0, 23)], send.at[1])
    await_bytes(s2buf.at[pl.ds(0, 3)], send.at[2])
    await_bytes(g4send, send.at[3])
    await_bytes(rs_send.at[pl.ds(0, 7)], send.at[4])
    await_bytes(g3buf.at[pl.ds(0, 15)], send.at[5])

    def sent(me, shards, src, slot):
        @pl.when(me < shards)
        def _():
            await_bytes(src.at[pl.ds(0, shards - 1)], send.at[slot])

        @pl.when(me >= shards)
        def _():
            await_bytes(src.at[pl.ds(0, shards)], send.at[slot])

    sent(sx, N4, a4, 8)
    sent(rank, N3, a3, 9)
    sent(rank, N2, a2, 11)

    @pl.when(sx < N4)
    def _():
        await_bytes(in4.at[pl.ds(0, 31)], send.at[10])

    @pl.when(rank < N3)
    def _():
        await_bytes(mid3.at[pl.ds(0, 7)], send.at[12])
        await_bytes(in3.at[pl.ds(0, 31)], send.at[14])

    @pl.when(rank < N2)
    def _():
        await_bytes(mid2.at[pl.ds(0, 7)], send.at[13])
        await_bytes(in2.at[pl.ds(0, 31)], send.at[15])


def per_device(volume, w_first, w_second, w_third, w_deep, grad_out):
    cells = 2 * lax.axis_size("sx") * 4 * 128
    scale = 1.0 / float(cells) ** 0.5
    vmem = pl.BlockSpec(memory_space=pltpu.VMEM)

    def kernel(*refs):
        whole_kernel(*refs, scale)

    outs = pl.pallas_call(
        kernel,
        out_shape=(
            jax.ShapeDtypeStruct((32, 1024), BF),
            jax.ShapeDtypeStruct((32, 108), F32),
            jax.ShapeDtypeStruct((64, 864), F32),
            jax.ShapeDtypeStruct((128, 1728), F32),
            jax.ShapeDtypeStruct((32, 3456), F32),
        ),
        in_specs=[vmem] * 8,
        out_specs=(vmem,) * 5,
        scratch_shapes=[
            pltpu.VMEM((512, 512), BF),
            pltpu.VMEM((96, 288), BF),
            pltpu.VMEM((512, 256), BF),
            pltpu.VMEM((256, 512), BF),
            pltpu.VMEM((896, 128), BF),
            pltpu.VMEM((128, 896), BF),
            pltpu.VMEM((64, 3456), BF),
            pltpu.VMEM((3, 64, 512), BF),
            pltpu.VMEM((288, 768), BF),
            pltpu.VMEM((64, 512), F32),
            pltpu.VMEM((864, 128), BF),
            pltpu.VMEM((24, 64, 128), BF),
            pltpu.VMEM((192, 36 * 128), BF),
            pltpu.VMEM((64, 128), F32),
            pltpu.VMEM((4, 64, 128), F32),
            pltpu.VMEM((8, 128, 128), F32),
            pltpu.VMEM((384, 24 * 128), BF),
            pltpu.VMEM((2, 32, 512), BF),
            pltpu.VMEM((2, 32, 512), BF),
            pltpu.VMEM((96, 24 * 128), BF),
            pltpu.VMEM((8, 128, 128), BF),
            pltpu.VMEM((8, 128, 128), BF),
            pltpu.VMEM((128, 128), BF),
            pltpu.VMEM((16, 128, 128), BF),
            pltpu.VMEM((384, 16 * 128), BF),
            pltpu.VMEM((512, 128), BF),
            pltpu.VMEM((N3, 64, 128), BF),
            pltpu.VMEM((N2, 16, 128), BF),
            pltpu.VMEM((N4, 32, 128), BF),
            pltpu.VMEM((32, 64, 128), BF),
            pltpu.VMEM((32, 16, 128), BF),
            pltpu.VMEM((32, 32, 128), BF),
            pltpu.VMEM((8, 64, 128), BF),
            pltpu.VMEM((8, 16, 128), BF),
            pltpu.VMEM((64, 128), BF),
            pltpu.VMEM((16, 128), BF),
            pltpu.VMEM((N3, 64, 128), BF),
            pltpu.VMEM((N2, 16, 128), BF),
            pltpu.VMEM((N4, 32, 128), BF),
            pltpu.SemaphoreType.DMA((16,)),
            pltpu.SemaphoreType.DMA((16,)),
        ],
        compiler_params=pltpu.CompilerParams(
            collective_id=1, has_side_effects=True, vmem_limit_bytes=48 * 1024 * 1024
        ),
        name="forward_and_backward",
    )(
        volume.reshape(64, 512),
        w_first,
        w_second,
        w_third,
        w_deep,
        grad_out.reshape(32, 1024),
        jnp.asarray(row_choice(), BF),
        jnp.asarray(band_choice(), BF),
    )
    activ, grad_w1, grad_w2, grad_w3, grad_w4 = outs
    return (activ.reshape(32, 2, 4, 128), grad_w1, grad_w2, grad_w3, grad_w4)


def solution(mesh):
    placed = (
        P(None, ("sx", "ch"), "sy", None),
        P(),
        P(),
        P(),
        P(("sy", "ch"), None),
        P(("sy", "ch"), "sx", None, None),
    )
    return jax.shard_map(
        per_device,
        mesh=mesh,
        in_specs=placed,
        out_specs=(P(("sy", "ch"), "sx", None, None), P(), P(), P(), P(("sy", "ch"), None)),
        check_vma=False,
    )
```

```python
import numpy as np
import jax
import jax.numpy as jnp
from jax import lax
from jax.experimental import pallas as pl
from jax.experimental.pallas import tpu as pltpu
from jax.sharding import PartitionSpec as P

MESH = pl.DeviceIdType.MESH
BF = jnp.bfloat16
F32 = jnp.float32
HALF = 14


def row_choice():
    pick = np.zeros((224, 256), np.float32)
    for d in range(7):
        for h in range(7):
            block = (0 if d >= 3 else 1) + (0 if h >= 3 else 2)
            for c in range(4):
                source = block * 64 + c * 16 + ((d + 1) % 4) * 4 + (h + 1) % 4
                pick[d * 32 + h * 4 + c, source] = 1.0
    return pick


def band_choice():
    pick = np.zeros((3, 128, 288), np.float32)
    for j in range(3):
        for kd in range(3):
            for kh in range(3):
                for kw in range(3):
                    for c in range(4):
                        pick[j, (9 * kd + 3 * kh + kw) * 4 + c, kw * 96 + kd * 32 + (2 * j + kh) * 4 + c] = 1.0
    return pick


def smooth_unit(values):
    return 0.3 * values + 0.7 * values * jax.nn.sigmoid(values)


def smooth_slope(values):
    sigma = jax.nn.sigmoid(values)
    return 0.3 + 0.7 * (sigma + values * sigma * (1.0 - sigma))


def mm(a, b):
    return jnp.dot(a, b, preferred_element_type=F32)


def mm_nt(a, b):
    return lax.dot_general(a, b, (((1,), (1,)), ((), ())), preferred_element_type=F32)


def lane_of(shape):
    return lax.broadcasted_iota(jnp.int32, shape, len(shape) - 1)


def from_left(x):
    return jnp.where(lane_of(x.shape) == 0, 0.0, pltpu.roll(x, 1, 1))


def from_right(x):
    return jnp.where(lane_of(x.shape) == 127, 0.0, pltpu.roll(x, 127, 1))


def await_bytes(ref, sem):
    pltpu.make_async_copy(ref, ref, sem).wait()


def whole_kernel(
    vol, w1, w2, w3t, w4, gout, rows_pick, band,
    activ, out2, out3, out4,
    perm, w1band, wbk_t, wbk, wb4_t, wb4, w3, w3b,
    vin, vst, p1, a1, gath, x2s, s2own, s2buf, p3, x3s,
    g4send, g4halo, g4s, rs_send, rs_recv, g3own, g3buf, g3s, g2st,
    a3, a2, a4, pair3, pair4, sum3, sum4, in3, in2, in4, mid3, mid2, part3, part2, all3, all2, all4,
    send, recv, scale,
):
    sx, sy, ch = lax.axis_index("sx"), lax.axis_index("sy"), lax.axis_index("ch")
    core = lax.rem(sx, 2)
    z = lax.rem(lax.div(sx, 2), 8)
    low = lax.div(sx, 16)
    rank = low * 16 + core * 8 + ch * 4 + sy
    rank3 = low * 8 + ch * 4 + sy
    rank4 = low * 8 + z
    g = sx * 2 + ch
    cell = ch * 4 + sy

    def block_place(depth_block, row_block):
        d = lax.rem(depth_block + 64, 64)
        return (lax.div(d, 2), lax.rem(row_block + 4, 4), lax.rem(d, 2))

    def wrap(value, size):
        return jnp.where(value >= size, value - size, value)

    xs = [sy] + [wrap(sy + k, 4) for k in (1, 2, 3)]
    chs = (ch, 1 - ch)
    cores = (core, 1 - core)
    lows = (low, 1 - low)
    groups = {-1: wrap(sx + 31, 32), 0: sx, 1: wrap(sx + 1, 32)}
    ring = (0, 1, 2, 1)

    near = []
    for far in range(4, -1, -1):
        for dg in (-1, 1, 0):
            for dx in range(4):
                for dc in range(2):
                    if ring[dx] + 2 * dc == far and (dg or dx or dc):
                        near.append((dg, (groups[dg], xs[dx], chs[dc])))
    plane = []
    mates = []
    for far in range(5, -1, -1):
        for dl in range(2):
            for dn in range(2):
                group = lows[dl] * 16 + z * 2 + cores[dn]
                first = lows[dl] * 16 + cores[dn] * 8
                for dx in range(4):
                    for dc in range(2):
                        if ring[dx] + 2 * dc + dl == far and (dl or dn or dx or dc):
                            entry = (first + chs[dc] * 4 + xs[dx], (group, xs[dx], chs[dc]))
                            plane.append(entry)
                            if dl or dn:
                                mates.append(entry)
    column = []
    for k in (4, 3, 5, 2, 6, 1, 7):
        other = wrap(z + k, 8)
        column.append((other, (low * 16 + other * 2 + core, sy, ch)))
    mate = (sx + 1 - 2 * core, sy, ch)
    square = []
    for far in range(5, -1, -1):
        for dl in range(2):
            for dx in range(4):
                for dc in range(2):
                    if ring[dx] + 2 * dc + dl == far and (dl or dx or dc):
                        other = lows[dl] * 8 + chs[dc] * 4 + xs[dx]
                        square.append((other, (lows[dl] * 16 + z * 2 + core, xs[dx], chs[dc])))
    line = []
    for k in (4, 3, 5, 2, 6, 1, 7, 0):
        for dl in (1, 0):
            if k or dl:
                there = wrap(z + k, 8)
                line.append((lows[dl] * 8 + there, (lows[dl] * 16 + there * 2 + core, sy, ch), k))
    beyond = [(other, place) for other, place, k in line if k]
    line = [(other, place) for other, place, k in line]

    def push(src, dst, slot, place):
        pltpu.make_async_remote_copy(
            src_ref=src, dst_ref=dst, send_sem=send.at[slot], recv_sem=recv.at[slot],
            device_id=place, device_id_type=MESH,
        ).start()

    barrier = pltpu.get_barrier_semaphore()

    for other, place in near + mates + beyond:
        pl.semaphore_signal(barrier, inc=1, device_id=place, device_id_type=MESH)

    for p in range(4):
        r = lax.broadcasted_iota(jnp.int32, (512, 128), 0)
        perm[:, p * 128 : (p + 1) * 128] = jnp.where(r == 4 * lane_of((512, 128)) + p, 1.0, 0.0).astype(BF)
    for j in range(3):
        w1band[j * 32 : (j + 1) * 32, :] = mm(w1[...], band[j, :108, :]).astype(BF)
    zero = jnp.zeros((96, 128), BF)
    for d in range(6):
        for h in (0, 5):
            at = (d * 6 + h) * 128
            for r in range(2):
                x2s[r * 96 : (r + 1) * 96, at : at + 128] = zero
            if d < 4:
                g4s[:, at : at + 128] = zero
                for r in range(4):
                    x3s[r * 96 : (r + 1) * 96, at : at + 128] = zero
    for t in range(27):
        wb4_t[t * 32 : (t + 1) * 32, :] = w4[:, (26 - t) * 128 : (27 - t) * 128]
    wb4_t[864:896, :] = jnp.zeros((32, 128), BF)
    a2[30] = jnp.zeros((16, 128), BF)
    a3[1, 13] = jnp.zeros((64, 128), BF)
    a4[1, 13] = jnp.zeros((32, 128), BF)
    a2[31] = jnp.zeros((16, 128), BF)
    for k in range(7):
        wb4[:, k * 128 : (k + 1) * 128] = wb4_t[k * 128 : (k + 1) * 128, :].astype(F32).T.astype(BF)
    for k in range(14):
        size = 128 if k < 13 else 64
        turned = w3t[k * 128 : k * 128 + size, :]
        w3[:, k * 128 : k * 128 + size] = turned.astype(F32).T.astype(BF)
    for t in range(27):
        w3b[:, (26 - t) * 128 : (27 - t) * 128] = w3t[t * 64 : (t + 1) * 64, :]
    wbk_t[...] = jnp.zeros((512, 256), BF)
    taps = {(0, 0): 1, (1, 0): 2, (1, 1): 0}
    for (pa, a), kd in taps.items():
        for (pb, b), kh in taps.items():
            for (pe, s), kw in taps.items():
                r = (a * 4 + b * 2 + s) * 64
                c = (pa * 4 + pe * 2 + pb) * 32
                t = (9 * kd + 3 * kh + kw) * 32
                wbk_t[r : r + 64, c : c + 32] = w2[:, t : t + 32]
    for r in range(4):
        for c in range(2):
            block = wbk_t[r * 128 : (r + 1) * 128, c * 128 : (c + 1) * 128]
            wbk[c * 128 : (c + 1) * 128, r * 128 : (r + 1) * 128] = block.astype(F32).T.astype(BF)

    pl.semaphore_wait(barrier, 23 + 24 + 14)

    push(vol, vin.at[0], 0, block_place(g + 1, sy))
    push(vol, vin.at[1], 0, block_place(g, sy + 1))
    push(vol, vin.at[2], 0, block_place(g + 1, sy + 1))

    await_bytes(vin, recv.at[0])
    none = jnp.zeros((64, 512), BF)
    blocks = jnp.concatenate(
        [
            vol[...],
            jnp.where(g > 0, vin[0], none),
            jnp.where(sy > 0, vin[1], none),
            jnp.where((g > 0) & (sy > 0), vin[2], none),
        ],
        axis=0,
    )
    ordered = mm(mm(rows_pick[...], blocks).astype(BF), perm[...])
    phases = [ordered[:, p * 128 : (p + 1) * 128] for p in range(4)]
    before = from_left(phases[3]).astype(BF)
    phases = [x.astype(BF) for x in phases]
    for q, used in enumerate(((before, phases[0], phases[1]), (phases[1], phases[2], phases[3]))):
        for kw in range(3):
            for i in range(3):
                at = (2 * i + q) * 128
                vst[kw * 96 : (kw + 1) * 96, at : at + 128] = used[kw][64 * i : 64 * i + 96]
    pre_one = mm(w1band[...], vst[...])
    p1[...] = pre_one[32:, 256:]
    act_one = smooth_unit(pre_one)
    for i in range(3):
        even = act_one[:, (2 * i) * 128 : (2 * i + 1) * 128]
        odd = act_one[:, (2 * i + 1) * 128 : (2 * i + 2) * 128]
        three = (from_left(odd).astype(BF), even.astype(BF), odd.astype(BF))
        for j in range(3):
            for kw in range(3):
                r = (3 * i + j) * 96 + kw * 32
                a1[r : r + 32, :] = three[kw][j * 32 : (j + 1) * 32]
    pre_two = mm(w2[...], a1[...])
    act_two = smooth_unit(pre_two).astype(BF)
    own = (ch + 2) * 4 + sy
    gath[own] = act_two

    for group, place in near:
        push(gath.at[own], gath.at[own - 8 * group], 1, place)
    slope_two = smooth_slope(pre_two)
    s2own[...] = slope_two
    s2buf[0] = slope_two
    push(s2own, s2buf.at[1], 2, block_place(g, sy - 1))
    push(s2own, s2buf.at[2], 2, block_place(g - 1, sy))
    push(s2own, s2buf.at[3], 2, block_place(g - 1, sy - 1))
    await_bytes(gath.at[pl.ds(0, 23)], recv.at[1])

    def spread_three(ref, rows, at, x, keep):
        if keep is not None:
            x = jnp.where(keep, x, 0.0)
        ref[0:rows, pl.ds(at, 128)] = from_left(x).astype(BF)
        ref[rows : 2 * rows, pl.ds(at, 128)] = x.astype(BF)
        ref[2 * rows : 3 * rows, pl.ds(at, 128)] = from_right(x).astype(BF)

    for d in range(6):
        keep = sx > 0 if d < 2 else (sx < 31 if d > 3 else None)
        for h in range(4):
            spread_three(x2s, 64, (d * 6 + h + 1) * 128, gath[d * 4 + h].astype(F32), keep)

    def taps_of(ref, p):
        return jnp.concatenate(
            [ref[:, ((p + kd) * 6 + kh) * 128 : ((p + kd) * 6 + kh + 4) * 128] for kd in range(3) for kh in range(3)],
            axis=0,
        )

    for p in range(4):
        pre = mm(w3[...], taps_of(x2s, p))
        act = smooth_unit(pre)
        keep = sx > 0 if p == 0 else (sx < 31 if p == 3 else None)
        for h in range(4):
            piece = slice(h * 128, (h + 1) * 128)
            if p in (1, 2):
                p3[(p - 1) * 4 + h] = pre[:, piece]
            spread_three(x3s, 128, (p * 6 + h + 1) * 128, act[:, piece].astype(BF).astype(F32), keep)

    grads = []
    for p in range(2):
        pre = mm(w4[...], taps_of(x3s, p))
        here = slice(p * 512, (p + 1) * 512)
        activ[:, here] = smooth_unit(pre).astype(BF)
        grad = (gout[:, here].astype(F32) * smooth_slope(pre) * scale).astype(BF)
        grads.append(grad)
        g4send[p] = grad
    push(g4send.at[0], g4halo.at[1], 3, (lax.rem(sx + 31, 32), sy, ch))
    push(g4send.at[1], g4halo.at[0], 3, (lax.rem(sx + 1, 32), sy, ch))
    for kd in range(3):
        for kh in range(3):
            part = None
            for p in range(2):
                at = ((p + kd) * 6 + kh) * 128
                more = mm_nt(grads[p], x3s[:, at : at + 512])
                part = more if part is None else part + more
            for kw in range(3):
                a4[(9 * kd + 3 * kh + kw) // HALF, (9 * kd + 3 * kh + kw) % HALF] = part[:, kw * 128 : (kw + 1) * 128].astype(BF)
    push(a4.at[1 - core], pair4, 16, mate)
    for p in range(2):
        for h in range(4):
            x = grads[p][:, h * 128 : (h + 1) * 128].astype(F32)
            spread_three(g4s, 32, ((p + 1) * 6 + h + 1) * 128, x, None)
    await_bytes(g4halo, recv.at[3])
    for e, p, keep in ((0, 0, sx > 0), (1, 3, sx < 31)):
        for h in range(4):
            x = g4halo[e, :, h * 128 : (h + 1) * 128].astype(F32)
            spread_three(g4s, 32, (p * 6 + h + 1) * 128, x, keep)
    for p in range(2):
        back = mm(wb4[:, :864], taps_of(g4s, p)).astype(BF)
        for h in range(4):
            rs_send[p * 4 + h] = back[:, h * 128 : (h + 1) * 128]

    for group, place in near:
        if place[0] is sx:
            push(rs_send.at[place[2] * 4 + place[1]], rs_recv.at[cell], 4, place)

    def scatter(places, shards, src, dst, mine, slot):
        for other, place in places:
            if shards == 32:
                push(src.at[other], dst.at[mine], slot, place)
            else:
                @pl.when(other < shards)
                def _():
                    push(src.at[other], dst.at[mine], slot, place)

    def spread(places, src, dst, slot):
        for other, place in places:
            push(src, dst, slot, place)

    def total(ref):
        return jnp.sum(ref[...].astype(F32), axis=0)

    await_bytes(pair4, recv.at[16])
    sum4[...] = (a4[core].astype(F32) + pair4[...].astype(F32)).astype(BF)
    scatter(line, HALF, sum4, in4, rank4, 8)
    rs_recv[cell] = rs_send[cell]
    await_bytes(rs_recv.at[pl.ds(0, 7)], recv.at[4])
    grad_three = (total(rs_recv) * smooth_slope(p3[cell])).astype(BF)
    g3own[...] = grad_three
    g3buf[5] = grad_three

    for up in (-1, 1, 2, 0):
        d = lax.rem(g - up + 64, 64)
        group, side_ch = lax.div(d, 2), lax.rem(d, 2)
        for side in (2, -1, 1, 0):
            if up or side:
                push(g3own, g3buf.at[(up + 1) * 4 + side + 1], 5, (group, xs[(-side) % 4], side_ch))

    for kd in range(3):
        for kh in range(3):
            at = pl.multiple_of(((ch + 1 + kd) * 6 + sy + kh) * 128, 128)
            part = mm_nt(x2s[:, pl.ds(at, 128)], grad_three).astype(BF)
            for kw in range(3):
                a3[(9 * kd + 3 * kh + kw) // HALF, (9 * kd + 3 * kh + kw) % HALF] = part[kw * 64 : (kw + 1) * 64]
    push(a3.at[1 - core], pair3, 6, mate)

    @pl.when(rank4 < HALF)
    def _():
        in4[rank4] = sum4[rank4]
        await_bytes(in4.at[pl.ds(0, 15)], recv.at[8])
        all4[core, rank4] = total(in4).astype(BF)
        spread(line, all4.at[core, rank4], all4.at[core, rank4], 10)

    await_bytes(pair3, recv.at[6])
    sum3[...] = (a3[core].astype(F32) + pair3[...].astype(F32)).astype(BF)
    scatter(square, HALF, sum3, in3, rank3, 9)

    await_bytes(g3buf.at[pl.ds(0, 15)], recv.at[5])
    for d in range(4):
        for h in range(4):
            keep = (g - 1 + d >= 0) & (g - 1 + d < 64) & (sy - 1 + h >= 0) & (sy - 1 + h < 4)
            spread_three(g3s, 128, (d * 4 + h) * 128, g3buf[d * 4 + h].astype(F32), keep)
    await_bytes(s2buf.at[pl.ds(0, 3)], recv.at[2])
    for a in range(2):
        around = jnp.concatenate(
            [g3s[:, ((a + kd) * 4 + kh) * 128 : ((a + kd) * 4 + kh + 2) * 128] for kd in range(3) for kh in range(3)],
            axis=0,
        )
        back = mm(w3b[...], around)
        for b in range(2):
            x = back[:, b * 128 : (b + 1) * 128] * s2buf[a * 2 + b]
            if a or b:
                keep = (g + a < 64) & (sy + b < 4)
                x = jnp.where(keep, x, 0.0)
            x = x.astype(BF)
            r = (a * 2 + b) * 128
            g2st[r : r + 64, :] = x
            g2st[r + 64 : r + 128, :] = from_right(x.astype(F32)).astype(BF)
    @pl.when(rank3 < HALF)
    def _():
        in3[rank3] = sum3[rank3]
        await_bytes(in3.at[pl.ds(0, 15)], recv.at[9])
        part3[...] = total(in3).astype(BF)
        mid3[z] = part3[...]
        spread(column, part3, mid3.at[z], 12)

    back_one = mm(wbk[...], g2st[...])
    slope_one = smooth_slope(p1[...])
    grad_one = jnp.concatenate(
        [back_one[k * 64 : (k + 1) * 64] * slope_one[:, k * 128 : (k + 1) * 128] for k in range(4)], axis=1
    ).astype(BF)
    banded = mm_nt(grad_one, vst[:, 256:])
    high = banded.astype(BF)
    rest = (banded - high.astype(F32)).astype(BF)
    local_one = jnp.zeros((32, 128), F32)
    for b in range(2):
        local_one += mm_nt(high[b * 32 : (b + 1) * 32], band[b + 1])
        local_one += mm_nt(rest[b * 32 : (b + 1) * 32], band[b + 1])
    local_one = local_one.astype(BF)
    a2[28] = local_one[:16]
    a2[29] = local_one[16:]
    grad_two = g2st[0:64, :]
    for k in range(7):
        size = 128 if k < 6 else 96
        part = mm_nt(grad_two, a1[k * 128 : k * 128 + size, :]).astype(BF)
        if k == 6:
            part = jnp.concatenate([part, jnp.zeros((64, 32), BF)], axis=1)
        for r in range(4):
            a2[k * 4 + r] = part[r * 16 : (r + 1) * 16]
    scatter(plane, 32, a2, in2, rank, 11)

    @pl.when(rank3 < HALF)
    def _():
        await_bytes(mid3.at[pl.ds(0, 7)], recv.at[12])
        all3[core, rank3] = total(mid3).astype(BF)
        spread(square, all3.at[core, rank3], all3.at[core, rank3], 14)

    in2[rank] = a2[rank]
    await_bytes(in2.at[pl.ds(0, 31)], recv.at[11])
    part2[...] = total(in2).astype(BF)
    mid2[z] = part2[...]
    spread(column, part2, mid2.at[z], 13)

    await_bytes(mid2.at[pl.ds(0, 7)], recv.at[13])
    all2[rank] = total(mid2).astype(BF)
    spread(plane, all2.at[rank], all2.at[rank], 15)

    def arrived(me, buf, slot):
        @pl.when(me < HALF)
        def _():
            await_bytes(buf.at[0, pl.ds(0, HALF - 1)], recv.at[slot])

        @pl.when(me >= HALF)
        def _():
            await_bytes(buf.at[0], recv.at[slot])

    arrived(rank4, all4, 10)
    push(all4.at[core], all4.at[core], 17, mate)
    arrived(rank3, all3, 14)
    push(all3.at[core], all3.at[core], 7, mate)
    await_bytes(all4.at[0], recv.at[17])
    out4[...] = all4[...]
    await_bytes(all3.at[0], recv.at[7])
    out3[...] = all3[...]
    await_bytes(all2.at[pl.ds(0, 31)], recv.at[15])
    out2[...] = all2[...]

    await_bytes(vin, send.at[0])
    await_bytes(gath.at[pl.ds(0, 23)], send.at[1])
    await_bytes(s2buf.at[pl.ds(0, 3)], send.at[2])
    await_bytes(g4send, send.at[3])
    await_bytes(rs_send.at[pl.ds(0, 7)], send.at[4])
    await_bytes(g3buf.at[pl.ds(0, 15)], send.at[5])

    await_bytes(in2.at[pl.ds(0, 31)], send.at[11])
    for pair, total_sum, gathered, slots in ((pair4, sum4, all4, (16, 8, 10, 17)), (pair3, sum3, all3, (6, 9, 14, 7))):
        me = rank4 if pair is pair4 else rank3
        await_bytes(pair, send.at[slots[0]])
        await_bytes(gathered.at[0], send.at[slots[3]])

        @pl.when(me < HALF)
        def _():
            await_bytes(total_sum.at[pl.ds(0, HALF - 1)], send.at[slots[1]])

        @pl.when(me >= HALF)
        def _():
            await_bytes(total_sum, send.at[slots[1]])

    @pl.when(rank4 < HALF)
    def _():
        await_bytes(in4.at[pl.ds(0, 15)], send.at[10])

    @pl.when(rank3 < HALF)
    def _():
        await_bytes(mid3.at[pl.ds(0, 7)], send.at[12])
        await_bytes(in3.at[pl.ds(0, 15)], send.at[14])

    await_bytes(mid2.at[pl.ds(0, 7)], send.at[13])
    await_bytes(in2.at[pl.ds(0, 31)], send.at[15])


def finish_kernel(act, all2, all3, all4, activ, o1, o2, o3, o4):
    for p in range(2):
        for h in range(4):
            at = (p * 4 + h) * 128
            activ[:, p, h, :] = act[:, at : at + 128]
    for t in range(27):
        o4[:, t * 128 : (t + 1) * 128] = all4[t // HALF, t % HALF].astype(F32)
        o3[t * 64 : (t + 1) * 64, :] = all3[t // HALF, t % HALF].astype(F32)
    for k in range(7):
        size = 128 if k < 6 else 96
        for r in range(4):
            o2[r * 16 : (r + 1) * 16, k * 128 : k * 128 + size] = all2[k * 4 + r].astype(F32)[:, :size]
    o1[0:16, :] = all2[28].astype(F32)[:, :108]
    o1[16:32, :] = all2[29].astype(F32)[:, :108]


def per_device(volume, w_first, w_second, w_third, w_deep, grad_out):
    cells = 2 * lax.axis_size("sx") * 4 * 128
    scale = 1.0 / float(cells) ** 0.5
    vmem = pl.BlockSpec(memory_space=pltpu.VMEM)

    def kernel(*refs):
        whole_kernel(*refs, scale)

    outs = pl.pallas_call(
        kernel,
        out_shape=(
            jax.ShapeDtypeStruct((32, 1024), BF),
            jax.ShapeDtypeStruct((32, 16, 128), BF),
            jax.ShapeDtypeStruct((2, HALF, 64, 128), BF),
            jax.ShapeDtypeStruct((2, HALF, 32, 128), BF),
        ),
        in_specs=[vmem] * 8,
        out_specs=(vmem,) * 4,
        scratch_shapes=[
            pltpu.VMEM((512, 512), BF),
            pltpu.VMEM((96, 288), BF),
            pltpu.VMEM((512, 256), BF),
            pltpu.VMEM((256, 512), BF),
            pltpu.VMEM((896, 128), BF),
            pltpu.VMEM((128, 896), BF),
            pltpu.VMEM((128, 1728), BF),
            pltpu.VMEM((64, 3456), BF),
            pltpu.VMEM((3, 64, 512), BF),
            pltpu.VMEM((288, 768), BF),
            pltpu.VMEM((64, 512), F32),
            pltpu.VMEM((864, 128), BF),
            pltpu.VMEM((24, 64, 128), BF),
            pltpu.VMEM((192, 36 * 128), BF),
            pltpu.VMEM((64, 128), F32),
            pltpu.VMEM((4, 64, 128), F32),
            pltpu.VMEM((8, 128, 128), F32),
            pltpu.VMEM((384, 24 * 128), BF),
            pltpu.VMEM((2, 32, 512), BF),
            pltpu.VMEM((2, 32, 512), BF),
            pltpu.VMEM((96, 24 * 128), BF),
            pltpu.VMEM((8, 128, 128), BF),
            pltpu.VMEM((8, 128, 128), BF),
            pltpu.VMEM((128, 128), BF),
            pltpu.VMEM((16, 128, 128), BF),
            pltpu.VMEM((384, 16 * 128), BF),
            pltpu.VMEM((512, 128), BF),
            pltpu.VMEM((2, HALF, 64, 128), BF),
            pltpu.VMEM((32, 16, 128), BF),
            pltpu.VMEM((2, HALF, 32, 128), BF),
            pltpu.VMEM((HALF, 64, 128), BF),
            pltpu.VMEM((HALF, 32, 128), BF),
            pltpu.VMEM((HALF, 64, 128), BF),
            pltpu.VMEM((HALF, 32, 128), BF),
            pltpu.VMEM((16, 64, 128), BF),
            pltpu.VMEM((32, 16, 128), BF),
            pltpu.VMEM((16, 32, 128), BF),
            pltpu.VMEM((8, 64, 128), BF),
            pltpu.VMEM((8, 16, 128), BF),
            pltpu.VMEM((64, 128), BF),
            pltpu.VMEM((16, 128), BF),
            pltpu.VMEM((2, HALF, 64, 128), BF),
            pltpu.VMEM((32, 16, 128), BF),
            pltpu.VMEM((2, HALF, 32, 128), BF),
            pltpu.SemaphoreType.DMA((18,)),
            pltpu.SemaphoreType.DMA((18,)),
        ],
        compiler_params=pltpu.CompilerParams(
            collective_id=1, has_side_effects=True, vmem_limit_bytes=48 * 1024 * 1024
        ),
        name="forward_and_backward",
    )(
        volume.reshape(64, 512),
        w_first,
        w_second,
        w_third.T,
        w_deep,
        grad_out.reshape(32, 1024),
        jnp.asarray(row_choice(), BF),
        jnp.asarray(band_choice(), BF),
    )
    activ, grad_w1, grad_w2, grad_w3, grad_w4 = pl.pallas_call(
        finish_kernel,
        out_shape=(
            jax.ShapeDtypeStruct((32, 2, 4, 128), BF),
            jax.ShapeDtypeStruct((32, 108), F32),
            jax.ShapeDtypeStruct((64, 864), F32),
            jax.ShapeDtypeStruct((1728, 128), F32),
            jax.ShapeDtypeStruct((32, 3456), F32),
        ),
        compiler_params=pltpu.CompilerParams(vmem_limit_bytes=32 * 1024 * 1024),
        name="widen_outputs",
    )(*outs)
    return (activ, grad_w1, grad_w2, grad_w3.T, grad_w4)


def solution(mesh):
    placed = (
        P(None, ("sx", "ch"), "sy", None),
        P(),
        P(),
        P(),
        P(("sy", "ch"), None),
        P(("sy", "ch"), "sx", None, None),
    )
    return jax.shard_map(
        per_device,
        mesh=mesh,
        in_specs=placed,
        out_specs=(P(("sy", "ch"), "sx", None, None), P(), P(), P(), P(("sy", "ch"), None)),
        check_vma=False,
    )
```

```python
import numpy as np
import jax
import jax.numpy as jnp
from jax import lax
from jax.experimental import pallas as pl
from jax.experimental.pallas import tpu as pltpu
from jax.sharding import PartitionSpec as P

MESH = pl.DeviceIdType.MESH
BF = jnp.bfloat16
F32 = jnp.float32
HALF = 14


def row_choice():
    pick = np.zeros((224, 256), np.float32)
    for d in range(7):
        for h in range(7):
            block = (0 if d >= 3 else 1) + (0 if h >= 3 else 2)
            for c in range(4):
                source = block * 64 + c * 16 + ((d + 1) % 4) * 4 + (h + 1) % 4
                pick[d * 32 + h * 4 + c, source] = 1.0
    return pick


def band_choice():
    pick = np.zeros((3, 128, 288), np.float32)
    for j in range(3):
        for kd in range(3):
            for kh in range(3):
                for kw in range(3):
                    for c in range(4):
                        pick[j, (9 * kd + 3 * kh + kw) * 4 + c, kw * 96 + kd * 32 + (2 * j + kh) * 4 + c] = 1.0
    return pick


def smooth_unit(values):
    return 0.3 * values + 0.7 * values * jax.nn.sigmoid(values)


def smooth_slope(values):
    sigma = jax.nn.sigmoid(values)
    return 0.3 + 0.7 * (sigma + values * sigma * (1.0 - sigma))


def mm(a, b):
    return jnp.dot(a, b, preferred_element_type=F32)


def mm_nt(a, b):
    return lax.dot_general(a, b, (((1,), (1,)), ((), ())), preferred_element_type=F32)


def lane_of(shape):
    return lax.broadcasted_iota(jnp.int32, shape, len(shape) - 1)


def from_left(x):
    return jnp.where(lane_of(x.shape) == 0, 0.0, pltpu.roll(x, 1, 1))


def from_right(x):
    return jnp.where(lane_of(x.shape) == 127, 0.0, pltpu.roll(x, 127, 1))


def await_bytes(ref, sem):
    pltpu.make_async_copy(ref, ref, sem).wait()


def whole_kernel(
    vol_in, w1_in, w2_in, w3t_in, w4_in, gout_in, rows_in, band_in,
    activ_out, out2, out3, out4,
    perm, w1band, wbk_t, wbk, wb4_t, wb4, w3, w3b,
    vin, vst, p1, a1, gath, x2s, s2own, s2buf, p3, x3s,
    g4send, g4halo, g4s, rs_send, rs_recv, g3own, g3buf, g3s, g2st,
    a3, a2, a4, pair3, pair4, sum3, sum4, in3, in2, in4, mid3, mid2, part3, part2, all3, all2, all4,
    activ, vol_raw, gout_raw, vol, w1, w2, w3t, w4, gout, rows_pick, band,
    send, recv, load, scale,
):
    sx, sy, ch = lax.axis_index("sx"), lax.axis_index("sy"), lax.axis_index("ch")
    core = lax.rem(sx, 2)
    z = lax.rem(lax.div(sx, 2), 8)
    low = lax.div(sx, 16)
    rank = low * 16 + core * 8 + ch * 4 + sy
    rank3 = low * 8 + ch * 4 + sy
    rank4 = low * 8 + z
    g = sx * 2 + ch
    cell = ch * 4 + sy

    def block_place(depth_block, row_block):
        d = lax.rem(depth_block + 64, 64)
        return (lax.div(d, 2), lax.rem(row_block + 4, 4), lax.rem(d, 2))

    def wrap(value, size):
        return jnp.where(value >= size, value - size, value)

    xs = [sy] + [wrap(sy + k, 4) for k in (1, 2, 3)]
    chs = (ch, 1 - ch)
    cores = (core, 1 - core)
    lows = (low, 1 - low)
    groups = {-1: wrap(sx + 31, 32), 0: sx, 1: wrap(sx + 1, 32)}
    ring = (0, 1, 2, 1)

    near = []
    for far in range(4, -1, -1):
        for dg in (-1, 1, 0):
            for dx in range(4):
                for dc in range(2):
                    if ring[dx] + 2 * dc == far and (dg or dx or dc):
                        near.append((dg, (groups[dg], xs[dx], chs[dc])))
    plane = []
    mates = []
    for far in range(5, -1, -1):
        for dl in range(2):
            for dn in range(2):
                group = lows[dl] * 16 + z * 2 + cores[dn]
                first = lows[dl] * 16 + cores[dn] * 8
                for dx in range(4):
                    for dc in range(2):
                        if ring[dx] + 2 * dc + dl == far and (dl or dn or dx or dc):
                            entry = (first + chs[dc] * 4 + xs[dx], (group, xs[dx], chs[dc]))
                            plane.append(entry)
                            if dl or dn:
                                mates.append(entry)
    column = []
    for k in (4, 3, 5, 2, 6, 1, 7):
        other = wrap(z + k, 8)
        column.append((other, (low * 16 + other * 2 + core, sy, ch)))
    mate = (sx + 1 - 2 * core, sy, ch)
    square = []
    for far in range(5, -1, -1):
        for dl in range(2):
            for dx in range(4):
                for dc in range(2):
                    if ring[dx] + 2 * dc + dl == far and (dl or dx or dc):
                        other = lows[dl] * 8 + chs[dc] * 4 + xs[dx]
                        square.append((other, (lows[dl] * 16 + z * 2 + core, xs[dx], chs[dc])))
    line = []
    for k in (4, 3, 5, 2, 6, 1, 7, 0):
        for dl in (1, 0):
            if k or dl:
                there = wrap(z + k, 8)
                line.append((lows[dl] * 8 + there, (lows[dl] * 16 + there * 2 + core, sy, ch), k))
    beyond = [(other, place) for other, place, k in line if k]
    line = [(other, place) for other, place, k in line]

    def push(src, dst, slot, place):
        pltpu.make_async_remote_copy(
            src_ref=src, dst_ref=dst, send_sem=send.at[slot], recv_sem=recv.at[slot],
            device_id=place, device_id_type=MESH,
        ).start()

    barrier = pltpu.get_barrier_semaphore()

    for other, place in near + mates + beyond:
        pl.semaphore_signal(barrier, inc=1, device_id=place, device_id_type=MESH)

    loads = [
        pltpu.make_async_copy(src, dst, load.at[k])
        for k, (src, dst) in enumerate(
            (
                (vol_in, vol_raw), (w1_in, w1), (band_in, band), (w4_in, w4), (w3t_in, w3t),
                (w2_in, w2), (rows_in, rows_pick), (gout_in, gout_raw),
            )
        )
    ]
    for each in loads:
        each.start()
    loads[0].wait()
    vol[...] = vol_raw[...].astype(F32).reshape(64, 512).astype(BF)
    pl.semaphore_wait(barrier, 23 + 24 + 14)

    push(vol, vin.at[0], 0, block_place(g + 1, sy))
    push(vol, vin.at[1], 0, block_place(g, sy + 1))
    push(vol, vin.at[2], 0, block_place(g + 1, sy + 1))

    for p in range(4):
        r = lax.broadcasted_iota(jnp.int32, (512, 128), 0)
        perm[:, p * 128 : (p + 1) * 128] = jnp.where(r == 4 * lane_of((512, 128)) + p, 1.0, 0.0).astype(BF)
    for each in loads[1:]:
        each.wait()
    for j in range(3):
        w1band[j * 32 : (j + 1) * 32, :] = mm(w1[...], band[j, :108, :]).astype(BF)
    zero = jnp.zeros((96, 128), BF)
    for d in range(6):
        for h in (0, 5):
            at = (d * 6 + h) * 128
            for r in range(2):
                x2s[r * 96 : (r + 1) * 96, at : at + 128] = zero
            if d < 4:
                g4s[:, at : at + 128] = zero
                for r in range(4):
                    x3s[r * 96 : (r + 1) * 96, at : at + 128] = zero
    for k in range(14):
        size = 128 if k < 13 else 64
        turned = w3t[k * 128 : k * 128 + size, :]
        w3[:, k * 128 : k * 128 + size] = turned.astype(F32).T.astype(BF)
    for p in range(2):
        for h in range(4):
            at = (p * 4 + h) * 128
            gout[:, at : at + 128] = gout_raw[:, p, h, :]
    await_bytes(vin, recv.at[0])
    none = jnp.zeros((64, 512), BF)
    blocks = jnp.concatenate(
        [
            vol[...],
            jnp.where(g > 0, vin[0], none),
            jnp.where(sy > 0, vin[1], none),
            jnp.where((g > 0) & (sy > 0), vin[2], none),
        ],
        axis=0,
    )
    ordered = mm(mm(rows_pick[...], blocks).astype(BF), perm[...])
    phases = [ordered[:, p * 128 : (p + 1) * 128] for p in range(4)]
    before = from_left(phases[3]).astype(BF)
    phases = [x.astype(BF) for x in phases]
    for q, used in enumerate(((before, phases[0], phases[1]), (phases[1], phases[2], phases[3]))):
        for kw in range(3):
            for i in range(3):
                at = (2 * i + q) * 128
                vst[kw * 96 : (kw + 1) * 96, at : at + 128] = used[kw][64 * i : 64 * i + 96]
    pre_one = mm(w1band[...], vst[...])
    p1[...] = pre_one[32:, 256:]
    act_one = smooth_unit(pre_one)
    for i in range(3):
        even = act_one[:, (2 * i) * 128 : (2 * i + 1) * 128]
        odd = act_one[:, (2 * i + 1) * 128 : (2 * i + 2) * 128]
        three = (from_left(odd).astype(BF), even.astype(BF), odd.astype(BF))
        for j in range(3):
            for kw in range(3):
                r = (3 * i + j) * 96 + kw * 32
                a1[r : r + 32, :] = three[kw][j * 32 : (j + 1) * 32]
    pre_two = mm(w2[...], a1[...])
    act_two = smooth_unit(pre_two).astype(BF)
    own = (ch + 2) * 4 + sy
    gath[own] = act_two

    for group, place in near:
        push(gath.at[own], gath.at[own - 8 * group], 1, place)
    slope_two = smooth_slope(pre_two)
    s2own[...] = slope_two
    s2buf[0] = slope_two
    push(s2own, s2buf.at[1], 2, block_place(g, sy - 1))
    push(s2own, s2buf.at[2], 2, block_place(g - 1, sy))
    push(s2own, s2buf.at[3], 2, block_place(g - 1, sy - 1))
    for t in range(27):
        wb4_t[t * 32 : (t + 1) * 32, :] = w4[:, (26 - t) * 128 : (27 - t) * 128]
    wb4_t[864:896, :] = jnp.zeros((32, 128), BF)
    a2[30] = jnp.zeros((16, 128), BF)
    a3[1, 13] = jnp.zeros((64, 128), BF)
    a4[1, 13] = jnp.zeros((32, 128), BF)
    a2[31] = jnp.zeros((16, 128), BF)
    for k in range(7):
        wb4[:, k * 128 : (k + 1) * 128] = wb4_t[k * 128 : (k + 1) * 128, :].astype(F32).T.astype(BF)
    for t in range(27):
        w3b[:, (26 - t) * 128 : (27 - t) * 128] = w3t[t * 64 : (t + 1) * 64, :]
    wbk_t[...] = jnp.zeros((512, 256), BF)
    taps = {(0, 0): 1, (1, 0): 2, (1, 1): 0}
    for (pa, a), kd in taps.items():
        for (pb, b), kh in taps.items():
            for (pe, s), kw in taps.items():
                r = (a * 4 + b * 2 + s) * 64
                c = (pa * 4 + pe * 2 + pb) * 32
                t = (9 * kd + 3 * kh + kw) * 32
                wbk_t[r : r + 64, c : c + 32] = w2[:, t : t + 32]
    for r in range(4):
        for c in range(2):
            block = wbk_t[r * 128 : (r + 1) * 128, c * 128 : (c + 1) * 128]
            wbk[c * 128 : (c + 1) * 128, r * 128 : (r + 1) * 128] = block.astype(F32).T.astype(BF)

    await_bytes(gath.at[pl.ds(0, 23)], recv.at[1])

    def spread_three(ref, rows, at, x, keep):
        if keep is not None:
            x = jnp.where(keep, x, 0.0)
        ref[0:rows, pl.ds(at, 128)] = from_left(x).astype(BF)
        ref[rows : 2 * rows, pl.ds(at, 128)] = x.astype(BF)
        ref[2 * rows : 3 * rows, pl.ds(at, 128)] = from_right(x).astype(BF)

    for d in range(6):
        keep = sx > 0 if d < 2 else (sx < 31 if d > 3 else None)
        for h in range(4):
            spread_three(x2s, 64, (d * 6 + h + 1) * 128, gath[d * 4 + h].astype(F32), keep)

    def taps_of(ref, p):
        return jnp.concatenate(
            [ref[:, ((p + kd) * 6 + kh) * 128 : ((p + kd) * 6 + kh + 4) * 128] for kd in range(3) for kh in range(3)],
            axis=0,
        )

    for p in range(4):
        pre = mm(w3[...], taps_of(x2s, p))
        act = smooth_unit(pre)
        keep = sx > 0 if p == 0 else (sx < 31 if p == 3 else None)
        for h in range(4):
            piece = slice(h * 128, (h + 1) * 128)
            if p in (1, 2):
                p3[(p - 1) * 4 + h] = pre[:, piece]
            spread_three(x3s, 128, (p * 6 + h + 1) * 128, act[:, piece].astype(BF).astype(F32), keep)

    grads = []
    for p in range(2):
        pre = mm(w4[...], taps_of(x3s, p))
        here = slice(p * 512, (p + 1) * 512)
        activ[:, here] = smooth_unit(pre).astype(BF)
        grad = (gout[:, here].astype(F32) * smooth_slope(pre) * scale).astype(BF)
        grads.append(grad)
        g4send[p] = grad
    stores = [
        pltpu.make_async_copy(src, dst, load.at[8 + k])
        for k, (src, dst) in enumerate(((activ, activ_out), (all4, out4), (all3, out3), (all2, out2)))
    ]
    push(g4send.at[0], g4halo.at[1], 3, (lax.rem(sx + 31, 32), sy, ch))
    push(g4send.at[1], g4halo.at[0], 3, (lax.rem(sx + 1, 32), sy, ch))
    for kd in range(3):
        for kh in range(3):
            part = None
            for p in range(2):
                at = ((p + kd) * 6 + kh) * 128
                more = mm_nt(grads[p], x3s[:, at : at + 512])
                part = more if part is None else part + more
            for kw in range(3):
                a4[(9 * kd + 3 * kh + kw) // HALF, (9 * kd + 3 * kh + kw) % HALF] = part[:, kw * 128 : (kw + 1) * 128].astype(BF)
    push(a4.at[1 - core], pair4, 16, mate)
    for p in range(2):
        for h in range(4):
            x = grads[p][:, h * 128 : (h + 1) * 128].astype(F32)
            spread_three(g4s, 32, ((p + 1) * 6 + h + 1) * 128, x, None)
    stores[0].start()
    await_bytes(g4halo, recv.at[3])
    for e, p, keep in ((0, 0, sx > 0), (1, 3, sx < 31)):
        for h in range(4):
            x = g4halo[e, :, h * 128 : (h + 1) * 128].astype(F32)
            spread_three(g4s, 32, (p * 6 + h + 1) * 128, x, keep)
    for p in range(2):
        back = mm(wb4[:, :864], taps_of(g4s, p)).astype(BF)
        for h in range(4):
            rs_send[p * 4 + h] = back[:, h * 128 : (h + 1) * 128]

    for group, place in near:
        if place[0] is sx:
            push(rs_send.at[place[2] * 4 + place[1]], rs_recv.at[cell], 4, place)

    def scatter(places, shards, src, dst, mine, slot):
        for other, place in places:
            if shards == 32:
                push(src.at[other], dst.at[mine], slot, place)
            else:
                @pl.when(other < shards)
                def _():
                    push(src.at[other], dst.at[mine], slot, place)

    def spread(places, src, dst, slot):
        for other, place in places:
            push(src, dst, slot, place)

    def total(ref):
        return jnp.sum(ref[...].astype(F32), axis=0)

    await_bytes(pair4, recv.at[16])
    sum4[...] = (a4[core].astype(F32) + pair4[...].astype(F32)).astype(BF)
    scatter(line, HALF, sum4, in4, rank4, 8)
    rs_recv[cell] = rs_send[cell]
    await_bytes(rs_recv.at[pl.ds(0, 7)], recv.at[4])
    grad_three = (total(rs_recv) * smooth_slope(p3[cell])).astype(BF)
    g3own[...] = grad_three
    g3buf[5] = grad_three

    for up in (-1, 1, 2, 0):
        d = lax.rem(g - up + 64, 64)
        group, side_ch = lax.div(d, 2), lax.rem(d, 2)
        for side in (2, -1, 1, 0):
            if up or side:
                push(g3own, g3buf.at[(up + 1) * 4 + side + 1], 5, (group, xs[(-side) % 4], side_ch))

    for kd in range(3):
        for kh in range(3):
            at = pl.multiple_of(((ch + 1 + kd) * 6 + sy + kh) * 128, 128)
            part = mm_nt(x2s[:, pl.ds(at, 128)], grad_three).astype(BF)
            for kw in range(3):
                a3[(9 * kd + 3 * kh + kw) // HALF, (9 * kd + 3 * kh + kw) % HALF] = part[kw * 64 : (kw + 1) * 64]
    push(a3.at[1 - core], pair3, 6, mate)

    @pl.when(rank4 < HALF)
    def _():
        in4[rank4] = sum4[rank4]
        await_bytes(in4.at[pl.ds(0, 15)], recv.at[8])
        all4[core, rank4] = total(in4).astype(BF)
        spread(line, all4.at[core, rank4], all4.at[core, rank4], 10)

    await_bytes(pair3, recv.at[6])
    sum3[...] = (a3[core].astype(F32) + pair3[...].astype(F32)).astype(BF)
    scatter(square, HALF, sum3, in3, rank3, 9)

    await_bytes(g3buf.at[pl.ds(0, 15)], recv.at[5])
    for d in range(4):
        for h in range(4):
            keep = (g - 1 + d >= 0) & (g - 1 + d < 64) & (sy - 1 + h >= 0) & (sy - 1 + h < 4)
            spread_three(g3s, 128, (d * 4 + h) * 128, g3buf[d * 4 + h].astype(F32), keep)
    await_bytes(s2buf.at[pl.ds(0, 3)], recv.at[2])
    for a in range(2):
        around = jnp.concatenate(
            [g3s[:, ((a + kd) * 4 + kh) * 128 : ((a + kd) * 4 + kh + 2) * 128] for kd in range(3) for kh in range(3)],
            axis=0,
        )
        back = mm(w3b[...], around)
        for b in range(2):
            x = back[:, b * 128 : (b + 1) * 128] * s2buf[a * 2 + b]
            if a or b:
                keep = (g + a < 64) & (sy + b < 4)
                x = jnp.where(keep, x, 0.0)
            x = x.astype(BF)
            r = (a * 2 + b) * 128
            g2st[r : r + 64, :] = x
            g2st[r + 64 : r + 128, :] = from_right(x.astype(F32)).astype(BF)
    @pl.when(rank3 < HALF)
    def _():
        in3[rank3] = sum3[rank3]
        await_bytes(in3.at[pl.ds(0, 15)], recv.at[9])
        part3[...] = total(in3).astype(BF)
        mid3[z] = part3[...]
        spread(column, part3, mid3.at[z], 12)

    back_one = mm(wbk[...], g2st[...])
    slope_one = smooth_slope(p1[...])
    grad_one = jnp.concatenate(
        [back_one[k * 64 : (k + 1) * 64] * slope_one[:, k * 128 : (k + 1) * 128] for k in range(4)], axis=1
    ).astype(BF)
    banded = mm_nt(grad_one, vst[:, 256:])
    high = banded.astype(BF)
    rest = (banded - high.astype(F32)).astype(BF)
    local_one = jnp.zeros((32, 128), F32)
    for b in range(2):
        local_one += mm_nt(high[b * 32 : (b + 1) * 32], band[b + 1])
        local_one += mm_nt(rest[b * 32 : (b + 1) * 32], band[b + 1])
    local_one = local_one.astype(BF)
    a2[28] = local_one[:16]
    a2[29] = local_one[16:]
    grad_two = g2st[0:64, :]
    for k in range(7):
        size = 128 if k < 6 else 96
        part = mm_nt(grad_two, a1[k * 128 : k * 128 + size, :]).astype(BF)
        if k == 6:
            part = jnp.concatenate([part, jnp.zeros((64, 32), BF)], axis=1)
        for r in range(4):
            a2[k * 4 + r] = part[r * 16 : (r + 1) * 16]
    scatter(plane, 32, a2, in2, rank, 11)

    @pl.when(rank3 < HALF)
    def _():
        await_bytes(mid3.at[pl.ds(0, 7)], recv.at[12])
        all3[core, rank3] = total(mid3).astype(BF)
        spread(square, all3.at[core, rank3], all3.at[core, rank3], 14)

    in2[rank] = a2[rank]
    await_bytes(in2.at[pl.ds(0, 31)], recv.at[11])
    part2[...] = total(in2).astype(BF)
    mid2[z] = part2[...]
    spread(column, part2, mid2.at[z], 13)

    await_bytes(mid2.at[pl.ds(0, 7)], recv.at[13])
    all2[rank] = total(mid2).astype(BF)
    spread(plane, all2.at[rank], all2.at[rank], 15)

    def arrived(me, buf, slot):
        @pl.when(me < HALF)
        def _():
            await_bytes(buf.at[0, pl.ds(0, HALF - 1)], recv.at[slot])

        @pl.when(me >= HALF)
        def _():
            await_bytes(buf.at[0], recv.at[slot])

    arrived(rank4, all4, 10)
    push(all4.at[core], all4.at[core], 17, mate)
    arrived(rank3, all3, 14)
    push(all3.at[core], all3.at[core], 7, mate)
    await_bytes(all4.at[0], recv.at[17])
    stores[1].start()
    await_bytes(all3.at[0], recv.at[7])
    stores[2].start()
    await_bytes(all2.at[pl.ds(0, 31)], recv.at[15])
    stores[3].start()

    for each in stores:
        each.wait()
    await_bytes(vin, send.at[0])
    await_bytes(gath.at[pl.ds(0, 23)], send.at[1])
    await_bytes(s2buf.at[pl.ds(0, 3)], send.at[2])
    await_bytes(g4send, send.at[3])
    await_bytes(rs_send.at[pl.ds(0, 7)], send.at[4])
    await_bytes(g3buf.at[pl.ds(0, 15)], send.at[5])

    await_bytes(in2.at[pl.ds(0, 31)], send.at[11])
    for pair, total_sum, gathered, slots in ((pair4, sum4, all4, (16, 8, 10, 17)), (pair3, sum3, all3, (6, 9, 14, 7))):
        me = rank4 if pair is pair4 else rank3
        await_bytes(pair, send.at[slots[0]])
        await_bytes(gathered.at[0], send.at[slots[3]])

        @pl.when(me < HALF)
        def _():
            await_bytes(total_sum.at[pl.ds(0, HALF - 1)], send.at[slots[1]])

        @pl.when(me >= HALF)
        def _():
            await_bytes(total_sum, send.at[slots[1]])

    @pl.when(rank4 < HALF)
    def _():
        await_bytes(in4.at[pl.ds(0, 15)], send.at[10])

    @pl.when(rank3 < HALF)
    def _():
        await_bytes(mid3.at[pl.ds(0, 7)], send.at[12])
        await_bytes(in3.at[pl.ds(0, 15)], send.at[14])

    await_bytes(mid2.at[pl.ds(0, 7)], send.at[13])
    await_bytes(in2.at[pl.ds(0, 31)], send.at[15])


def finish_kernel(act, all2, all3, all4, activ, o1, o2, o3, o4):
    for p in range(2):
        for h in range(4):
            at = (p * 4 + h) * 128
            activ[:, p, h, :] = act[:, at : at + 128]
    for t in range(27):
        o4[:, t * 128 : (t + 1) * 128] = all4[t // HALF, t % HALF].astype(F32)
        o3[t * 64 : (t + 1) * 64, :] = all3[t // HALF, t % HALF].astype(F32)
    for k in range(7):
        size = 128 if k < 6 else 96
        for r in range(4):
            o2[r * 16 : (r + 1) * 16, k * 128 : k * 128 + size] = all2[k * 4 + r].astype(F32)[:, :size]
    o1[0:16, :] = all2[28].astype(F32)[:, :108]
    o1[16:32, :] = all2[29].astype(F32)[:, :108]


def per_device(volume, w_first, w_second, w_third, w_deep, grad_out):
    cells = 2 * lax.axis_size("sx") * 4 * 128
    scale = 1.0 / float(cells) ** 0.5
    vmem = pl.BlockSpec(memory_space=pltpu.VMEM)

    def kernel(*refs):
        whole_kernel(*refs, scale)

    outs = pl.pallas_call(
        kernel,
        out_shape=(
            jax.ShapeDtypeStruct((32, 1024), BF),
            jax.ShapeDtypeStruct((32, 16, 128), BF),
            jax.ShapeDtypeStruct((2, HALF, 64, 128), BF),
            jax.ShapeDtypeStruct((2, HALF, 32, 128), BF),
        ),
        in_specs=[pl.BlockSpec(memory_space=pltpu.HBM)] * 8,
        out_specs=(pl.BlockSpec(memory_space=pltpu.HBM),) * 4,
        scratch_shapes=[
            pltpu.VMEM((512, 512), BF),
            pltpu.VMEM((96, 288), BF),
            pltpu.VMEM((512, 256), BF),
            pltpu.VMEM((256, 512), BF),
            pltpu.VMEM((896, 128), BF),
            pltpu.VMEM((128, 896), BF),
            pltpu.VMEM((128, 1728), BF),
            pltpu.VMEM((64, 3456), BF),
            pltpu.VMEM((3, 64, 512), BF),
            pltpu.VMEM((288, 768), BF),
            pltpu.VMEM((64, 512), F32),
            pltpu.VMEM((864, 128), BF),
            pltpu.VMEM((24, 64, 128), BF),
            pltpu.VMEM((192, 36 * 128), BF),
            pltpu.VMEM((64, 128), F32),
            pltpu.VMEM((4, 64, 128), F32),
            pltpu.VMEM((8, 128, 128), F32),
            pltpu.VMEM((384, 24 * 128), BF),
            pltpu.VMEM((2, 32, 512), BF),
            pltpu.VMEM((2, 32, 512), BF),
            pltpu.VMEM((96, 24 * 128), BF),
            pltpu.VMEM((8, 128, 128), BF),
            pltpu.VMEM((8, 128, 128), BF),
            pltpu.VMEM((128, 128), BF),
            pltpu.VMEM((16, 128, 128), BF),
            pltpu.VMEM((384, 16 * 128), BF),
            pltpu.VMEM((512, 128), BF),
            pltpu.VMEM((2, HALF, 64, 128), BF),
            pltpu.VMEM((32, 16, 128), BF),
            pltpu.VMEM((2, HALF, 32, 128), BF),
            pltpu.VMEM((HALF, 64, 128), BF),
            pltpu.VMEM((HALF, 32, 128), BF),
            pltpu.VMEM((HALF, 64, 128), BF),
            pltpu.VMEM((HALF, 32, 128), BF),
            pltpu.VMEM((16, 64, 128), BF),
            pltpu.VMEM((32, 16, 128), BF),
            pltpu.VMEM((16, 32, 128), BF),
            pltpu.VMEM((8, 64, 128), BF),
            pltpu.VMEM((8, 16, 128), BF),
            pltpu.VMEM((64, 128), BF),
            pltpu.VMEM((16, 128), BF),
            pltpu.VMEM((2, HALF, 64, 128), BF),
            pltpu.VMEM((32, 16, 128), BF),
            pltpu.VMEM((2, HALF, 32, 128), BF),
            pltpu.VMEM((32, 1024), BF),
            pltpu.VMEM((4, 4, 4, 512), BF),
            pltpu.VMEM((32, 2, 4, 128), BF),
            pltpu.VMEM((64, 512), BF),
            pltpu.VMEM((32, 108), BF),
            pltpu.VMEM((64, 864), BF),
            pltpu.VMEM((1728, 128), BF),
            pltpu.VMEM((32, 3456), BF),
            pltpu.VMEM((32, 1024), BF),
            pltpu.VMEM((224, 256), BF),
            pltpu.VMEM((3, 128, 288), BF),
            pltpu.SemaphoreType.DMA((18,)),
            pltpu.SemaphoreType.DMA((18,)),
            pltpu.SemaphoreType.DMA((12,)),
        ],
        compiler_params=pltpu.CompilerParams(
            collective_id=1, has_side_effects=True, vmem_limit_bytes=60 * 1024 * 1024
        ),
        name="forward_and_backward",
    )(
        volume,
        w_first,
        w_second,
        w_third.T,
        w_deep,
        grad_out,
        jnp.asarray(row_choice(), BF),
        jnp.asarray(band_choice(), BF),
    )
    activ, grad_w1, grad_w2, grad_w3, grad_w4 = pl.pallas_call(
        finish_kernel,
        out_shape=(
            jax.ShapeDtypeStruct((32, 2, 4, 128), BF),
            jax.ShapeDtypeStruct((32, 108), F32),
            jax.ShapeDtypeStruct((64, 864), F32),
            jax.ShapeDtypeStruct((1728, 128), F32),
            jax.ShapeDtypeStruct((32, 3456), F32),
        ),
        compiler_params=pltpu.CompilerParams(vmem_limit_bytes=60 * 1024 * 1024),
        name="widen_outputs",
    )(*outs)
    return (activ, grad_w1, grad_w2, grad_w3.T, grad_w4)


def solution(mesh):
    placed = (
        P(None, ("sx", "ch"), "sy", None),
        P(),
        P(),
        P(),
        P(("sy", "ch"), None),
        P(("sy", "ch"), "sx", None, None),
    )
    return jax.shard_map(
        per_device,
        mesh=mesh,
        in_specs=placed,
        out_specs=(P(("sy", "ch"), "sx", None, None), P(), P(), P(), P(("sy", "ch"), None)),
        check_vma=False,
    )
```

```python
import numpy as np
import jax
import jax.numpy as jnp
from jax import lax
from jax.experimental import pallas as pl
from jax.experimental.pallas import tpu as pltpu
from jax.sharding import PartitionSpec as P

MESH = pl.DeviceIdType.MESH
BF = jnp.bfloat16
F32 = jnp.float32
HALF = 14
SMALL = 30


def row_choice():
    pick = np.zeros((224, 256), np.float32)
    for d in range(7):
        for h in range(7):
            block = (0 if d >= 3 else 1) + (0 if h >= 3 else 2)
            for c in range(4):
                source = block * 64 + c * 16 + ((d + 1) % 4) * 4 + (h + 1) % 4
                pick[d * 32 + h * 4 + c, source] = 1.0
    return pick


def band_choice():
    pick = np.zeros((3, 128, 288), np.float32)
    for j in range(3):
        for kd in range(3):
            for kh in range(3):
                for kw in range(3):
                    for c in range(4):
                        pick[j, (9 * kd + 3 * kh + kw) * 4 + c, kw * 96 + kd * 32 + (2 * j + kh) * 4 + c] = 1.0
    return pick


def smooth_unit(values):
    return 0.3 * values + 0.7 * values * jax.nn.sigmoid(values)


def smooth_slope(values):
    sigma = jax.nn.sigmoid(values)
    return 0.3 + 0.7 * (sigma + values * sigma * (1.0 - sigma))


def mm(a, b):
    return jnp.dot(a, b, preferred_element_type=F32)


def mm_nt(a, b):
    return lax.dot_general(a, b, (((1,), (1,)), ((), ())), preferred_element_type=F32)


def lane_of(shape):
    return lax.broadcasted_iota(jnp.int32, shape, len(shape) - 1)


def from_left(x):
    return jnp.where(lane_of(x.shape) == 0, 0.0, pltpu.roll(x, 1, 1))


def from_right(x):
    return jnp.where(lane_of(x.shape) == 127, 0.0, pltpu.roll(x, 127, 1))


def await_bytes(ref, sem):
    pltpu.make_async_copy(ref, ref, sem).wait()


def whole_kernel(
    vol_in, w1_in, w2_in, w3t_in, w4_in, gout_in, rows_in, band_in,
    activ_out, out2, out3, out4,
    perm, w1band, wbk_t, wbk, wb4_t, wb4, w3, w3b,
    vin, vst, p1, a1, gath, x2s, s2own, s2buf, p3, x3s,
    g4send, g4halo, g4s, rs_send, rs_recv, g3own, g3buf, g3s, g2st,
    a3, a2, a4, pair3, pair4, sum3, sum4, in3, in2, in4, mid3, mid2, part3, part2, all3, all2, all4,
    activ, vol_raw, gout_raw, vol, w1, w2, w3t, w4, gout, rows_pick, band,
    send, recv, load, scale,
):
    sx, sy, ch = lax.axis_index("sx"), lax.axis_index("sy"), lax.axis_index("ch")
    core = lax.rem(sx, 2)
    z = lax.rem(lax.div(sx, 2), 8)
    low = lax.div(sx, 16)
    rank = low * 16 + core * 8 + ch * 4 + sy
    rank3 = low * 8 + ch * 4 + sy
    rank4 = low * 8 + z
    g = sx * 2 + ch
    cell = ch * 4 + sy

    def block_place(depth_block, row_block):
        d = lax.rem(depth_block + 64, 64)
        return (lax.div(d, 2), lax.rem(row_block + 4, 4), lax.rem(d, 2))

    def wrap(value, size):
        return jnp.where(value >= size, value - size, value)

    xs = [sy] + [wrap(sy + k, 4) for k in (1, 2, 3)]
    chs = (ch, 1 - ch)
    cores = (core, 1 - core)
    lows = (low, 1 - low)
    groups = {-1: wrap(sx + 31, 32), 0: sx, 1: wrap(sx + 1, 32)}
    ring = (0, 1, 2, 1)

    near = []
    for far in range(4, -1, -1):
        for dg in (-1, 1, 0):
            for dx in range(4):
                for dc in range(2):
                    if ring[dx] + 2 * dc == far and (dg or dx or dc):
                        near.append((dg, (groups[dg], xs[dx], chs[dc])))
    plane = []
    mates = []
    for far in range(5, -1, -1):
        for dl in range(2):
            for dn in range(2):
                group = lows[dl] * 16 + z * 2 + cores[dn]
                first = lows[dl] * 16 + cores[dn] * 8
                for dx in range(4):
                    for dc in range(2):
                        if ring[dx] + 2 * dc + dl == far and (dl or dn or dx or dc):
                            entry = (first + chs[dc] * 4 + xs[dx], (group, xs[dx], chs[dc]))
                            plane.append(entry)
                            if dl or dn:
                                mates.append(entry)
    column = []
    for k in (4, 3, 5, 2, 6, 1, 7):
        other = wrap(z + k, 8)
        column.append((other, (low * 16 + other * 2 + core, sy, ch)))
    mate = (sx + 1 - 2 * core, sy, ch)
    square = []
    for far in range(5, -1, -1):
        for dl in range(2):
            for dx in range(4):
                for dc in range(2):
                    if ring[dx] + 2 * dc + dl == far and (dl or dx or dc):
                        other = lows[dl] * 8 + chs[dc] * 4 + xs[dx]
                        square.append((other, (lows[dl] * 16 + z * 2 + core, xs[dx], chs[dc])))
    line = []
    for k in (4, 3, 5, 2, 6, 1, 7, 0):
        for dl in (1, 0):
            if k or dl:
                there = wrap(z + k, 8)
                line.append((lows[dl] * 8 + there, (lows[dl] * 16 + there * 2 + core, sy, ch), k))
    beyond = [(other, place) for other, place, k in line if k]
    line = [(other, place) for other, place, k in line]

    def push(src, dst, slot, place):
        pltpu.make_async_remote_copy(
            src_ref=src, dst_ref=dst, send_sem=send.at[slot], recv_sem=recv.at[slot],
            device_id=place, device_id_type=MESH,
        ).start()

    barrier = pltpu.get_barrier_semaphore()

    for other, place in near + mates + beyond:
        pl.semaphore_signal(barrier, inc=1, device_id=place, device_id_type=MESH)

    loads = [
        pltpu.make_async_copy(src, dst, load.at[k])
        for k, (src, dst) in enumerate(
            (
                (vol_in, vol_raw), (w1_in, w1), (band_in, band), (w4_in, w4), (w3t_in, w3t),
                (w2_in, w2), (rows_in, rows_pick), (gout_in, gout_raw),
            )
        )
    ]
    for each in loads:
        each.start()
    loads[0].wait()
    vol[...] = vol_raw[...].astype(F32).reshape(64, 512).astype(BF)
    pl.semaphore_wait(barrier, 23 + 24 + 14)

    push(vol, vin.at[0], 0, block_place(g + 1, sy))
    push(vol, vin.at[1], 0, block_place(g, sy + 1))
    push(vol, vin.at[2], 0, block_place(g + 1, sy + 1))

    for p in range(4):
        r = lax.broadcasted_iota(jnp.int32, (512, 128), 0)
        perm[:, p * 128 : (p + 1) * 128] = jnp.where(r == 4 * lane_of((512, 128)) + p, 1.0, 0.0).astype(BF)
    for each in loads[1:]:
        each.wait()
    for j in range(3):
        w1band[j * 32 : (j + 1) * 32, :] = mm(w1[...], band[j, :108, :]).astype(BF)
    zero = jnp.zeros((96, 128), BF)
    for d in range(6):
        for h in (0, 5):
            at = (d * 6 + h) * 128
            for r in range(2):
                x2s[r * 96 : (r + 1) * 96, at : at + 128] = zero
            if d < 4:
                g4s[:, at : at + 128] = zero
                for r in range(4):
                    x3s[r * 96 : (r + 1) * 96, at : at + 128] = zero
    for k in range(14):
        size = 128 if k < 13 else 64
        turned = w3t[k * 128 : k * 128 + size, :]
        w3[:, k * 128 : k * 128 + size] = turned.astype(F32).T.astype(BF)
    for p in range(2):
        for h in range(4):
            at = (p * 4 + h) * 128
            gout[:, at : at + 128] = gout_raw[:, p, h, :]
    await_bytes(vin, recv.at[0])
    none = jnp.zeros((64, 512), BF)
    blocks = jnp.concatenate(
        [
            vol[...],
            jnp.where(g > 0, vin[0], none),
            jnp.where(sy > 0, vin[1], none),
            jnp.where((g > 0) & (sy > 0), vin[2], none),
        ],
        axis=0,
    )
    ordered = mm(mm(rows_pick[...], blocks).astype(BF), perm[...])
    phases = [ordered[:, p * 128 : (p + 1) * 128] for p in range(4)]
    before = from_left(phases[3]).astype(BF)
    phases = [x.astype(BF) for x in phases]
    for q, used in enumerate(((before, phases[0], phases[1]), (phases[1], phases[2], phases[3]))):
        for kw in range(3):
            for i in range(3):
                at = (2 * i + q) * 128
                vst[kw * 96 : (kw + 1) * 96, at : at + 128] = used[kw][64 * i : 64 * i + 96]
    pre_one = mm(w1band[...], vst[...])
    p1[...] = pre_one[32:, 256:]
    act_one = smooth_unit(pre_one)
    for i in range(3):
        even = act_one[:, (2 * i) * 128 : (2 * i + 1) * 128]
        odd = act_one[:, (2 * i + 1) * 128 : (2 * i + 2) * 128]
        three = (from_left(odd).astype(BF), even.astype(BF), odd.astype(BF))
        for j in range(3):
            for kw in range(3):
                r = (3 * i + j) * 96 + kw * 32
                a1[r : r + 32, :] = three[kw][j * 32 : (j + 1) * 32]
    pre_two = mm(w2[...], a1[...])
    act_two = smooth_unit(pre_two).astype(BF)
    own = (ch + 2) * 4 + sy
    gath[own] = act_two

    for group, place in near:
        push(gath.at[own], gath.at[own - 8 * group], 1, place)
    slope_two = smooth_slope(pre_two)
    s2own[...] = slope_two
    s2buf[0] = slope_two
    push(s2own, s2buf.at[1], 2, block_place(g, sy - 1))
    push(s2own, s2buf.at[2], 2, block_place(g - 1, sy))
    push(s2own, s2buf.at[3], 2, block_place(g - 1, sy - 1))
    for t in range(27):
        wb4_t[t * 32 : (t + 1) * 32, :] = w4[:, (26 - t) * 128 : (27 - t) * 128]
    wb4_t[864:896, :] = jnp.zeros((32, 128), BF)
    all2[30] = jnp.zeros((16, 128), BF)
    a3[1, 13] = jnp.zeros((64, 128), BF)
    a4[1, 13] = jnp.zeros((32, 128), BF)
    all2[31] = jnp.zeros((16, 128), BF)
    for k in range(7):
        wb4[:, k * 128 : (k + 1) * 128] = wb4_t[k * 128 : (k + 1) * 128, :].astype(F32).T.astype(BF)
    for t in range(27):
        w3b[:, (26 - t) * 128 : (27 - t) * 128] = w3t[t * 64 : (t + 1) * 64, :]
    wbk_t[...] = jnp.zeros((512, 256), BF)
    taps = {(0, 0): 1, (1, 0): 2, (1, 1): 0}
    for (pa, a), kd in taps.items():
        for (pb, b), kh in taps.items():
            for (pe, s), kw in taps.items():
                r = (a * 4 + b * 2 + s) * 64
                c = (pa * 4 + pe * 2 + pb) * 32
                t = (9 * kd + 3 * kh + kw) * 32
                wbk_t[r : r + 64, c : c + 32] = w2[:, t : t + 32]
    for r in range(4):
        for c in range(2):
            block = wbk_t[r * 128 : (r + 1) * 128, c * 128 : (c + 1) * 128]
            wbk[c * 128 : (c + 1) * 128, r * 128 : (r + 1) * 128] = block.astype(F32).T.astype(BF)

    await_bytes(gath.at[pl.ds(0, 23)], recv.at[1])

    def spread_three(ref, rows, at, x, keep):
        if keep is not None:
            x = jnp.where(keep, x, 0.0)
        ref[0:rows, pl.ds(at, 128)] = from_left(x).astype(BF)
        ref[rows : 2 * rows, pl.ds(at, 128)] = x.astype(BF)
        ref[2 * rows : 3 * rows, pl.ds(at, 128)] = from_right(x).astype(BF)

    for d in range(6):
        keep = sx > 0 if d < 2 else (sx < 31 if d > 3 else None)
        for h in range(4):
            spread_three(x2s, 64, (d * 6 + h + 1) * 128, gath[d * 4 + h].astype(F32), keep)

    def taps_of(ref, p):
        return jnp.concatenate(
            [ref[:, ((p + kd) * 6 + kh) * 128 : ((p + kd) * 6 + kh + 4) * 128] for kd in range(3) for kh in range(3)],
            axis=0,
        )

    for p in range(4):
        pre = mm(w3[...], taps_of(x2s, p))
        act = smooth_unit(pre)
        keep = sx > 0 if p == 0 else (sx < 31 if p == 3 else None)
        for h in range(4):
            piece = slice(h * 128, (h + 1) * 128)
            if p in (1, 2):
                p3[(p - 1) * 4 + h] = pre[:, piece]
            spread_three(x3s, 128, (p * 6 + h + 1) * 128, act[:, piece].astype(BF).astype(F32), keep)

    grads = []
    for p in range(2):
        pre = mm(w4[...], taps_of(x3s, p))
        here = slice(p * 512, (p + 1) * 512)
        activ[:, here] = smooth_unit(pre).astype(BF)
        grad = (gout[:, here].astype(F32) * smooth_slope(pre) * scale).astype(BF)
        grads.append(grad)
        g4send[p] = grad
    stores = [
        pltpu.make_async_copy(src, dst, load.at[8 + k])
        for k, (src, dst) in enumerate(((activ, activ_out), (all4, out4), (all3, out3), (all2, out2)))
    ]
    push(g4send.at[0], g4halo.at[1], 3, (lax.rem(sx + 31, 32), sy, ch))
    push(g4send.at[1], g4halo.at[0], 3, (lax.rem(sx + 1, 32), sy, ch))
    for kd in range(3):
        for kh in range(3):
            part = None
            for p in range(2):
                at = ((p + kd) * 6 + kh) * 128
                more = mm_nt(grads[p], x3s[:, at : at + 512])
                part = more if part is None else part + more
            for kw in range(3):
                a4[(9 * kd + 3 * kh + kw) // HALF, (9 * kd + 3 * kh + kw) % HALF] = part[:, kw * 128 : (kw + 1) * 128].astype(BF)
    push(a4.at[1 - core], pair4, 16, mate)
    for p in range(2):
        for h in range(4):
            x = grads[p][:, h * 128 : (h + 1) * 128].astype(F32)
            spread_three(g4s, 32, ((p + 1) * 6 + h + 1) * 128, x, None)
    stores[0].start()
    await_bytes(g4halo, recv.at[3])
    for e, p, keep in ((0, 0, sx > 0), (1, 3, sx < 31)):
        for h in range(4):
            x = g4halo[e, :, h * 128 : (h + 1) * 128].astype(F32)
            spread_three(g4s, 32, (p * 6 + h + 1) * 128, x, keep)
    for p in range(2):
        back = mm(wb4[:, :864], taps_of(g4s, p)).astype(BF)
        for h in range(4):
            rs_send[p * 4 + h] = back[:, h * 128 : (h + 1) * 128]

    for group, place in near:
        if place[0] is sx:
            push(rs_send.at[place[2] * 4 + place[1]], rs_recv.at[cell], 4, place)

    def scatter(places, shards, src, dst, mine, slot):
        for other, place in places:
            if shards == 32:
                push(src.at[other], dst.at[mine], slot, place)
            else:
                @pl.when(other < shards)
                def _():
                    push(src.at[other], dst.at[mine], slot, place)

    def spread(places, src, dst, slot):
        for other, place in places:
            push(src, dst, slot, place)

    def total(ref):
        return jnp.sum(ref[...].astype(F32), axis=0)

    await_bytes(pair4, recv.at[16])
    sum4[...] = (a4[core].astype(F32) + pair4[...].astype(F32)).astype(BF)
    scatter(line, HALF, sum4, in4, rank4, 8)
    slope_three = smooth_slope(p3[cell])
    rs_recv[cell] = rs_send[cell]
    await_bytes(rs_recv.at[pl.ds(0, 7)], recv.at[4])
    grad_three = (total(rs_recv) * slope_three).astype(BF)
    g3own[...] = grad_three
    g3buf[5] = grad_three

    for up in (-1, 1, 2, 0):
        d = lax.rem(g - up + 64, 64)
        group, side_ch = lax.div(d, 2), lax.rem(d, 2)
        for side in (2, -1, 1, 0):
            if up or side:
                push(g3own, g3buf.at[(up + 1) * 4 + side + 1], 5, (group, xs[(-side) % 4], side_ch))

    for kd in range(3):
        for kh in range(3):
            at = pl.multiple_of(((ch + 1 + kd) * 6 + sy + kh) * 128, 128)
            part = mm_nt(x2s[:, pl.ds(at, 128)], grad_three).astype(BF)
            for kw in range(3):
                a3[(9 * kd + 3 * kh + kw) // HALF, (9 * kd + 3 * kh + kw) % HALF] = part[kw * 64 : (kw + 1) * 64]
    push(a3.at[1 - core], pair3, 6, mate)

    @pl.when(rank4 < HALF)
    def _():
        in4[rank4] = sum4[rank4]
        await_bytes(in4.at[pl.ds(0, 15)], recv.at[8])
        all4[core, rank4] = total(in4).astype(BF)
        spread(line, all4.at[core, rank4], all4.at[core, rank4], 10)

    await_bytes(pair3, recv.at[6])
    sum3[...] = (a3[core].astype(F32) + pair3[...].astype(F32)).astype(BF)
    scatter(square, HALF, sum3, in3, rank3, 9)

    p1[...] = smooth_slope(p1[...])
    await_bytes(g3buf.at[pl.ds(0, 15)], recv.at[5])
    for d in range(4):
        for h in range(4):
            keep = (g - 1 + d >= 0) & (g - 1 + d < 64) & (sy - 1 + h >= 0) & (sy - 1 + h < 4)
            spread_three(g3s, 128, (d * 4 + h) * 128, g3buf[d * 4 + h].astype(F32), keep)
    await_bytes(s2buf.at[pl.ds(0, 3)], recv.at[2])
    for a in range(2):
        around = jnp.concatenate(
            [g3s[:, ((a + kd) * 4 + kh) * 128 : ((a + kd) * 4 + kh + 2) * 128] for kd in range(3) for kh in range(3)],
            axis=0,
        )
        back = mm(w3b[...], around)
        for b in range(2):
            x = back[:, b * 128 : (b + 1) * 128] * s2buf[a * 2 + b]
            if a or b:
                keep = (g + a < 64) & (sy + b < 4)
                x = jnp.where(keep, x, 0.0)
            x = x.astype(BF)
            r = (a * 2 + b) * 128
            g2st[r : r + 64, :] = x
            g2st[r + 64 : r + 128, :] = from_right(x.astype(F32)).astype(BF)
    grad_two = g2st[0:64, :]
    for k in range(7):
        size = 128 if k < 6 else 96
        part = mm_nt(grad_two, a1[k * 128 : k * 128 + size, :]).astype(BF)
        if k == 6:
            part = jnp.concatenate([part, jnp.zeros((64, 32), BF)], axis=1)
        for r in range(4):
            a2[k * 4 + r] = part[r * 16 : (r + 1) * 16]
    scatter(plane, 28, a2, in2, rank, 11)
    back_one = mm(wbk[...], g2st[...])
    grad_one = jnp.concatenate(
        [back_one[k * 64 : (k + 1) * 64] * p1[:, k * 128 : (k + 1) * 128] for k in range(4)], axis=1
    ).astype(BF)
    banded = mm_nt(grad_one, vst[:, 256:])
    high = banded.astype(BF)
    rest = (banded - high.astype(F32)).astype(BF)
    local_one = jnp.zeros((32, 128), F32)
    for b in range(2):
        local_one += mm_nt(high[b * 32 : (b + 1) * 32], band[b + 1])
        local_one += mm_nt(rest[b * 32 : (b + 1) * 32], band[b + 1])
    local_one = local_one.astype(BF)
    a2[28] = local_one[:16]
    a2[29] = local_one[16:]
    for shard, row in ((28, 0), (29, 1)):
        @pl.when(rank != shard)
        def _():
            push(a2.at[shard], in2.at[rank], 11, (17 + z * 2, row, 1))
    @pl.when(rank3 < HALF)
    def _():
        in3[rank3] = sum3[rank3]
        await_bytes(in3.at[pl.ds(0, 15)], recv.at[9])
        part3[...] = total(in3).astype(BF)
        mid3[z] = part3[...]
        spread(column, part3, mid3.at[z], 12)

    @pl.when(rank < SMALL)
    def _():
        in2[rank] = a2[rank]
        await_bytes(in2.at[pl.ds(0, 31)], recv.at[11])
        part2[...] = total(in2).astype(BF)
        mid2[z] = part2[...]
        spread(column, part2, mid2.at[z], 13)

    @pl.when(rank3 < HALF)
    def _():
        await_bytes(mid3.at[pl.ds(0, 7)], recv.at[12])
        all3[core, rank3] = total(mid3).astype(BF)
        spread(square, all3.at[core, rank3], all3.at[core, rank3], 14)

    @pl.when(rank < SMALL)
    def _():
        await_bytes(mid2.at[pl.ds(0, 7)], recv.at[13])
        all2[rank] = total(mid2).astype(BF)
        spread(plane, all2.at[rank], all2.at[rank], 15)

    def arrived(me, buf, slot):
        @pl.when(me < HALF)
        def _():
            await_bytes(buf.at[0, pl.ds(0, HALF - 1)], recv.at[slot])

        @pl.when(me >= HALF)
        def _():
            await_bytes(buf.at[0], recv.at[slot])

    arrived(rank4, all4, 10)
    push(all4.at[core], all4.at[core], 17, mate)
    arrived(rank3, all3, 14)
    push(all3.at[core], all3.at[core], 7, mate)
    await_bytes(all4.at[0], recv.at[17])
    stores[1].start()
    await_bytes(all3.at[0], recv.at[7])
    stores[2].start()
    @pl.when(rank < SMALL)
    def _():
        await_bytes(all2.at[pl.ds(0, SMALL - 1)], recv.at[15])

    @pl.when(rank >= SMALL)
    def _():
        await_bytes(all2.at[pl.ds(0, SMALL)], recv.at[15])

    stores[3].start()

    for each in stores:
        each.wait()
    await_bytes(vin, send.at[0])
    await_bytes(gath.at[pl.ds(0, 23)], send.at[1])
    await_bytes(s2buf.at[pl.ds(0, 3)], send.at[2])
    await_bytes(g4send, send.at[3])
    await_bytes(rs_send.at[pl.ds(0, 7)], send.at[4])
    await_bytes(g3buf.at[pl.ds(0, 15)], send.at[5])

    @pl.when(rank < SMALL)
    def _():
        await_bytes(a2.at[pl.ds(0, SMALL - 1)], send.at[11])
        await_bytes(mid2.at[pl.ds(0, 7)], send.at[13])
        await_bytes(in2.at[pl.ds(0, 31)], send.at[15])

    @pl.when(rank >= SMALL)
    def _():
        await_bytes(a2.at[pl.ds(0, SMALL)], send.at[11])

    for pair, total_sum, gathered, slots in ((pair4, sum4, all4, (16, 8, 10, 17)), (pair3, sum3, all3, (6, 9, 14, 7))):
        me = rank4 if pair is pair4 else rank3
        await_bytes(pair, send.at[slots[0]])
        await_bytes(gathered.at[0], send.at[slots[3]])

        @pl.when(me < HALF)
        def _():
            await_bytes(total_sum.at[pl.ds(0, HALF - 1)], send.at[slots[1]])

        @pl.when(me >= HALF)
        def _():
            await_bytes(total_sum, send.at[slots[1]])

    @pl.when(rank4 < HALF)
    def _():
        await_bytes(in4.at[pl.ds(0, 15)], send.at[10])

    @pl.when(rank3 < HALF)
    def _():
        await_bytes(mid3.at[pl.ds(0, 7)], send.at[12])
        await_bytes(in3.at[pl.ds(0, 15)], send.at[14])


def finish_kernel(
    act_in, in2, in3, in4, activ_out, out1, out2, out3, out4,
    act, all2, all3, all4, activ, o1, o2, o3, o4, come, leave,
):
    loads = [
        pltpu.make_async_copy(src, dst, come.at[k])
        for k, (src, dst) in enumerate(((in4, all4), (in3, all3), (act_in, act), (in2, all2)))
    ]
    stores = [
        pltpu.make_async_copy(src, dst, leave.at[k])
        for k, (src, dst) in enumerate(
            ((o4, out4), (o3, out3), (activ, activ_out), (o2, out2), (o1, out1))
        )
    ]
    for each in loads:
        each.start()
    loads[0].wait()
    for t in range(27):
        o4[:, t * 128 : (t + 1) * 128] = all4[t // HALF, t % HALF].astype(F32)
    stores[0].start()
    loads[1].wait()
    for t in range(27):
        o3[t * 64 : (t + 1) * 64, :] = all3[t // HALF, t % HALF].astype(F32)
    stores[1].start()
    loads[2].wait()
    for p in range(2):
        for h in range(4):
            at = (p * 4 + h) * 128
            activ[:, p, h, :] = act[:, at : at + 128]
    stores[2].start()
    loads[3].wait()
    for k in range(7):
        size = 128 if k < 6 else 96
        for r in range(4):
            o2[r * 16 : (r + 1) * 16, k * 128 : k * 128 + size] = all2[k * 4 + r].astype(F32)[:, :size]
    stores[3].start()
    o1[0:16, :] = all2[28].astype(F32)[:, :108]
    o1[16:32, :] = all2[29].astype(F32)[:, :108]
    stores[4].start()
    for each in stores:
        each.wait()


def per_device(volume, w_first, w_second, w_third, w_deep, grad_out):
    cells = 2 * lax.axis_size("sx") * 4 * 128
    scale = 1.0 / float(cells) ** 0.5
    vmem = pl.BlockSpec(memory_space=pltpu.VMEM)

    def kernel(*refs):
        whole_kernel(*refs, scale)

    outs = pl.pallas_call(
        kernel,
        out_shape=(
            jax.ShapeDtypeStruct((32, 1024), BF),
            jax.ShapeDtypeStruct((32, 16, 128), BF),
            jax.ShapeDtypeStruct((2, HALF, 64, 128), BF),
            jax.ShapeDtypeStruct((2, HALF, 32, 128), BF),
        ),
        in_specs=[pl.BlockSpec(memory_space=pltpu.HBM)] * 8,
        out_specs=(pl.BlockSpec(memory_space=pltpu.HBM),) * 4,
        scratch_shapes=[
            pltpu.VMEM((512, 512), BF),
            pltpu.VMEM((96, 288), BF),
            pltpu.VMEM((512, 256), BF),
            pltpu.VMEM((256, 512), BF),
            pltpu.VMEM((896, 128), BF),
            pltpu.VMEM((128, 896), BF),
            pltpu.VMEM((128, 1728), BF),
            pltpu.VMEM((64, 3456), BF),
            pltpu.VMEM((3, 64, 512), BF),
            pltpu.VMEM((288, 768), BF),
            pltpu.VMEM((64, 512), F32),
            pltpu.VMEM((864, 128), BF),
            pltpu.VMEM((24, 64, 128), BF),
            pltpu.VMEM((192, 36 * 128), BF),
            pltpu.VMEM((64, 128), F32),
            pltpu.VMEM((4, 64, 128), F32),
            pltpu.VMEM((8, 128, 128), F32),
            pltpu.VMEM((384, 24 * 128), BF),
            pltpu.VMEM((2, 32, 512), BF),
            pltpu.VMEM((2, 32, 512), BF),
            pltpu.VMEM((96, 24 * 128), BF),
            pltpu.VMEM((8, 128, 128), BF),
            pltpu.VMEM((8, 128, 128), BF),
            pltpu.VMEM((128, 128), BF),
            pltpu.VMEM((16, 128, 128), BF),
            pltpu.VMEM((384, 16 * 128), BF),
            pltpu.VMEM((512, 128), BF),
            pltpu.VMEM((2, HALF, 64, 128), BF),
            pltpu.VMEM((32, 16, 128), BF),
            pltpu.VMEM((2, HALF, 32, 128), BF),
            pltpu.VMEM((HALF, 64, 128), BF),
            pltpu.VMEM((HALF, 32, 128), BF),
            pltpu.VMEM((HALF, 64, 128), BF),
            pltpu.VMEM((HALF, 32, 128), BF),
            pltpu.VMEM((16, 64, 128), BF),
            pltpu.VMEM((32, 16, 128), BF),
            pltpu.VMEM((16, 32, 128), BF),
            pltpu.VMEM((8, 64, 128), BF),
            pltpu.VMEM((8, 16, 128), BF),
            pltpu.VMEM((64, 128), BF),
            pltpu.VMEM((16, 128), BF),
            pltpu.VMEM((2, HALF, 64, 128), BF),
            pltpu.VMEM((32, 16, 128), BF),
            pltpu.VMEM((2, HALF, 32, 128), BF),
            pltpu.VMEM((32, 1024), BF),
            pltpu.VMEM((4, 4, 4, 512), BF),
            pltpu.VMEM((32, 2, 4, 128), BF),
            pltpu.VMEM((64, 512), BF),
            pltpu.VMEM((32, 108), BF),
            pltpu.VMEM((64, 864), BF),
            pltpu.VMEM((1728, 128), BF),
            pltpu.VMEM((32, 3456), BF),
            pltpu.VMEM((32, 1024), BF),
            pltpu.VMEM((224, 256), BF),
            pltpu.VMEM((3, 128, 288), BF),
            pltpu.SemaphoreType.DMA((18,)),
            pltpu.SemaphoreType.DMA((18,)),
            pltpu.SemaphoreType.DMA((12,)),
        ],
        compiler_params=pltpu.CompilerParams(
            collective_id=1, has_side_effects=True, vmem_limit_bytes=60 * 1024 * 1024
        ),
        name="forward_and_backward",
    )(
        volume,
        w_first,
        w_second,
        w_third.T,
        w_deep,
        grad_out,
        jnp.asarray(row_choice(), BF),
        jnp.asarray(band_choice(), BF),
    )
    activ, grad_w1, grad_w2, grad_w3, grad_w4 = pl.pallas_call(
        finish_kernel,
        out_shape=(
            jax.ShapeDtypeStruct((32, 2, 4, 128), BF),
            jax.ShapeDtypeStruct((32, 108), F32),
            jax.ShapeDtypeStruct((64, 864), F32),
            jax.ShapeDtypeStruct((1728, 128), F32),
            jax.ShapeDtypeStruct((32, 3456), F32),
        ),
        in_specs=[pl.BlockSpec(memory_space=pltpu.HBM)] * 4,
        out_specs=(pl.BlockSpec(memory_space=pltpu.HBM),) * 5,
        scratch_shapes=[
            pltpu.VMEM((32, 1024), BF),
            pltpu.VMEM((32, 16, 128), BF),
            pltpu.VMEM((2, HALF, 64, 128), BF),
            pltpu.VMEM((2, HALF, 32, 128), BF),
            pltpu.VMEM((32, 2, 4, 128), BF),
            pltpu.VMEM((32, 108), F32),
            pltpu.VMEM((64, 864), F32),
            pltpu.VMEM((1728, 128), F32),
            pltpu.VMEM((32, 3456), F32),
            pltpu.SemaphoreType.DMA((4,)),
            pltpu.SemaphoreType.DMA((5,)),
        ],
        compiler_params=pltpu.CompilerParams(vmem_limit_bytes=60 * 1024 * 1024),
        name="widen_outputs",
    )(*outs)
    return (activ, grad_w1, grad_w2, grad_w3.T, grad_w4)


def solution(mesh):
    placed = (
        P(None, ("sx", "ch"), "sy", None),
        P(),
        P(),
        P(),
        P(("sy", "ch"), None),
        P(("sy", "ch"), "sx", None, None),
    )
    return jax.shard_map(
        per_device,
        mesh=mesh,
        in_specs=placed,
        out_specs=(P(("sy", "ch"), "sx", None, None), P(), P(), P(), P(("sy", "ch"), None)),
        check_vma=False,
    )
```

```python
import numpy as np
import jax
import jax.numpy as jnp
from jax import lax
from jax.experimental import pallas as pl
from jax.experimental.pallas import tpu as pltpu
from jax.sharding import PartitionSpec as P

MESH = pl.DeviceIdType.MESH
BF = jnp.bfloat16
F32 = jnp.float32
HALF = 14
SMALL = 30


def row_choice():
    pick = np.zeros((224, 256), np.float32)
    for d in range(7):
        for h in range(7):
            block = (0 if d >= 3 else 1) + (0 if h >= 3 else 2)
            for c in range(4):
                source = block * 64 + c * 16 + ((d + 1) % 4) * 4 + (h + 1) % 4
                pick[d * 32 + h * 4 + c, source] = 1.0
    return pick


def band_choice():
    pick = np.zeros((3, 128, 288), np.float32)
    for j in range(3):
        for kd in range(3):
            for kh in range(3):
                for kw in range(3):
                    for c in range(4):
                        pick[j, (9 * kd + 3 * kh + kw) * 4 + c, kw * 96 + kd * 32 + (2 * j + kh) * 4 + c] = 1.0
    return pick


def smooth_unit(values):
    return 0.3 * values + 0.7 * values * jax.nn.sigmoid(values)


def smooth_slope(values):
    sigma = jax.nn.sigmoid(values)
    return 0.3 + 0.7 * (sigma + values * sigma * (1.0 - sigma))


def mm(a, b):
    return jnp.dot(a, b, preferred_element_type=F32)


def mm_nt(a, b):
    return lax.dot_general(a, b, (((1,), (1,)), ((), ())), preferred_element_type=F32)


def lane_of(shape):
    return lax.broadcasted_iota(jnp.int32, shape, len(shape) - 1)


def from_left(x):
    return jnp.where(lane_of(x.shape) == 0, 0.0, pltpu.roll(x, 1, 1))


def from_right(x):
    return jnp.where(lane_of(x.shape) == 127, 0.0, pltpu.roll(x, 127, 1))


def await_bytes(ref, sem):
    pltpu.make_async_copy(ref, ref, sem).wait()


def whole_kernel(
    vol_in, w1_in, w2_in, w3t_in, w4_in, gout_in, rows_in, band_in,
    activ_out, out2, out3, out4,
    perm, w1band, wbk_t, wbk, wb4_t, wb4, w3, w3b,
    vin, vst, p1, a1, gath, x2s, s2own, s2buf, p3, x3s,
    g4send, g4halo, g4s, rs_send, rs_recv, g3own, g3buf, g3s, g2st,
    a3, a2, a4, pair3, pair4, sum3, sum4, in3, in2, in4, mid3, mid2, part3, part2, all3, all2, all4,
    activ, vol_raw, gout_raw, vol, w1, w2, w3t, w4, gout, rows_pick, band,
    send, recv, load, scale,
):
    sx, sy, ch = lax.axis_index("sx"), lax.axis_index("sy"), lax.axis_index("ch")
    core = lax.rem(sx, 2)
    z = lax.rem(lax.div(sx, 2), 8)
    low = lax.div(sx, 16)
    rank = low * 16 + core * 8 + ch * 4 + sy
    rank3 = low * 8 + ch * 4 + sy
    rank4 = low * 8 + z
    g = sx * 2 + ch
    cell = ch * 4 + sy

    def block_place(depth_block, row_block):
        d = lax.rem(depth_block + 64, 64)
        return (lax.div(d, 2), lax.rem(row_block + 4, 4), lax.rem(d, 2))

    def wrap(value, size):
        return jnp.where(value >= size, value - size, value)

    xs = [sy] + [wrap(sy + k, 4) for k in (1, 2, 3)]
    chs = (ch, 1 - ch)
    cores = (core, 1 - core)
    lows = (low, 1 - low)
    groups = {-1: wrap(sx + 31, 32), 0: sx, 1: wrap(sx + 1, 32)}
    ring = (0, 1, 2, 1)

    near = []
    for far in range(4, -1, -1):
        for dg in (-1, 1, 0):
            for dx in range(4):
                for dc in range(2):
                    if ring[dx] + 2 * dc == far and (dg or dx or dc):
                        near.append((dg, (groups[dg], xs[dx], chs[dc])))
    plane = []
    mates = []
    for far in range(5, -1, -1):
        for dl in range(2):
            for dn in range(2):
                group = lows[dl] * 16 + z * 2 + cores[dn]
                first = lows[dl] * 16 + cores[dn] * 8
                for dx in range(4):
                    for dc in range(2):
                        if ring[dx] + 2 * dc + dl == far and (dl or dn or dx or dc):
                            entry = (first + chs[dc] * 4 + xs[dx], (group, xs[dx], chs[dc]))
                            plane.append(entry)
                            if dl or dn:
                                mates.append(entry)
    column = []
    for k in (4, 3, 5, 2, 6, 1, 7):
        other = wrap(z + k, 8)
        column.append((other, (low * 16 + other * 2 + core, sy, ch)))
    mate = (sx + 1 - 2 * core, sy, ch)
    square = []
    for far in range(5, -1, -1):
        for dl in range(2):
            for dx in range(4):
                for dc in range(2):
                    if ring[dx] + 2 * dc + dl == far and (dl or dx or dc):
                        other = lows[dl] * 8 + chs[dc] * 4 + xs[dx]
                        square.append((other, (lows[dl] * 16 + z * 2 + core, xs[dx], chs[dc])))
    line = []
    for k in (4, 3, 5, 2, 6, 1, 7, 0):
        for dl in (1, 0):
            if k or dl:
                there = wrap(z + k, 8)
                line.append((lows[dl] * 8 + there, (lows[dl] * 16 + there * 2 + core, sy, ch), k))
    beyond = [(other, place) for other, place, k in line if k]
    line = [(other, place) for other, place, k in line]

    def push(src, dst, slot, place):
        pltpu.make_async_remote_copy(
            src_ref=src, dst_ref=dst, send_sem=send.at[slot], recv_sem=recv.at[slot],
            device_id=place, device_id_type=MESH,
        ).start()

    barrier = pltpu.get_barrier_semaphore()

    for other, place in near + mates + beyond:
        pl.semaphore_signal(barrier, inc=1, device_id=place, device_id_type=MESH)

    loads = [
        pltpu.make_async_copy(src, dst, load.at[k])
        for k, (src, dst) in enumerate(
            (
                (vol_in, vol_raw), (w1_in, w1), (band_in, band), (w4_in, w4), (w3t_in, w3t),
                (w2_in, w2), (rows_in, rows_pick), (gout_in, gout_raw),
            )
        )
    ]
    for each in loads:
        each.start()
    loads[0].wait()
    vol[...] = vol_raw[...].astype(F32).reshape(64, 512).astype(BF)
    pl.semaphore_wait(barrier, 23 + 24 + 14)

    push(vol, vin.at[0], 0, block_place(g + 1, sy))
    push(vol, vin.at[1], 0, block_place(g, sy + 1))
    push(vol, vin.at[2], 0, block_place(g + 1, sy + 1))

    for p in range(4):
        r = lax.broadcasted_iota(jnp.int32, (512, 128), 0)
        perm[:, p * 128 : (p + 1) * 128] = jnp.where(r == 4 * lane_of((512, 128)) + p, 1.0, 0.0).astype(BF)
    for each in loads[1:]:
        each.wait()
    for j in range(3):
        w1band[j * 32 : (j + 1) * 32, :] = mm(w1[...], band[j, :108, :]).astype(BF)
    zero = jnp.zeros((96, 128), BF)
    for d in range(6):
        for h in (0, 5):
            at = (d * 6 + h) * 128
            for r in range(2):
                x2s[r * 96 : (r + 1) * 96, at : at + 128] = zero
            if d < 4:
                g4s[:, at : at + 128] = zero
                for r in range(4):
                    x3s[r * 96 : (r + 1) * 96, at : at + 128] = zero
    for k in range(14):
        size = 128 if k < 13 else 64
        turned = w3t[k * 128 : k * 128 + size, :]
        w3[:, k * 128 : k * 128 + size] = turned.astype(F32).T.astype(BF)
    for p in range(2):
        for h in range(4):
            at = (p * 4 + h) * 128
            gout[:, at : at + 128] = gout_raw[:, p, h, :]
    await_bytes(vin, recv.at[0])
    none = jnp.zeros((64, 512), BF)
    blocks = jnp.concatenate(
        [
            vol[...],
            jnp.where(g > 0, vin[0], none),
            jnp.where(sy > 0, vin[1], none),
            jnp.where((g > 0) & (sy > 0), vin[2], none),
        ],
        axis=0,
    )
    ordered = mm(mm(rows_pick[...], blocks).astype(BF), perm[...])
    phases = [ordered[:, p * 128 : (p + 1) * 128] for p in range(4)]
    before = from_left(phases[3]).astype(BF)
    phases = [x.astype(BF) for x in phases]
    for q, used in enumerate(((before, phases[0], phases[1]), (phases[1], phases[2], phases[3]))):
        for kw in range(3):
            for i in range(3):
                at = (2 * i + q) * 128
                vst[kw * 96 : (kw + 1) * 96, at : at + 128] = used[kw][64 * i : 64 * i + 96]
    pre_one = mm(w1band[...], vst[...])
    p1[...] = pre_one[32:, 256:]
    act_one = smooth_unit(pre_one)
    for i in range(3):
        even = act_one[:, (2 * i) * 128 : (2 * i + 1) * 128]
        odd = act_one[:, (2 * i + 1) * 128 : (2 * i + 2) * 128]
        three = (from_left(odd).astype(BF), even.astype(BF), odd.astype(BF))
        for j in range(3):
            for kw in range(3):
                r = (3 * i + j) * 96 + kw * 32
                a1[r : r + 32, :] = three[kw][j * 32 : (j + 1) * 32]
    pre_two = mm(w2[...], a1[...])
    act_two = smooth_unit(pre_two).astype(BF)
    own = (ch + 2) * 4 + sy
    gath[own] = act_two

    for group, place in near:
        push(gath.at[own], gath.at[own - 8 * group], 1, place)
    slope_two = smooth_slope(pre_two)
    s2own[...] = slope_two
    s2buf[0] = slope_two
    push(s2own, s2buf.at[1], 2, block_place(g, sy - 1))
    push(s2own, s2buf.at[2], 2, block_place(g - 1, sy))
    push(s2own, s2buf.at[3], 2, block_place(g - 1, sy - 1))
    for t in range(27):
        wb4_t[t * 32 : (t + 1) * 32, :] = w4[:, (26 - t) * 128 : (27 - t) * 128]
    wb4_t[864:896, :] = jnp.zeros((32, 128), BF)
    all2[30] = jnp.zeros((16, 128), BF)
    a3[1, 13] = jnp.zeros((64, 128), BF)
    a4[1, 13] = jnp.zeros((32, 128), BF)
    all2[31] = jnp.zeros((16, 128), BF)
    for k in range(7):
        wb4[:, k * 128 : (k + 1) * 128] = wb4_t[k * 128 : (k + 1) * 128, :].astype(F32).T.astype(BF)
    for t in range(27):
        w3b[:, (26 - t) * 128 : (27 - t) * 128] = w3t[t * 64 : (t + 1) * 64, :]
    wbk_t[...] = jnp.zeros((512, 256), BF)
    taps = {(0, 0): 1, (1, 0): 2, (1, 1): 0}
    for (pa, a), kd in taps.items():
        for (pb, b), kh in taps.items():
            for (pe, s), kw in taps.items():
                r = (a * 4 + b * 2 + s) * 64
                c = (pa * 4 + pe * 2 + pb) * 32
                t = (9 * kd + 3 * kh + kw) * 32
                wbk_t[r : r + 64, c : c + 32] = w2[:, t : t + 32]
    for r in range(4):
        for c in range(2):
            block = wbk_t[r * 128 : (r + 1) * 128, c * 128 : (c + 1) * 128]
            wbk[c * 128 : (c + 1) * 128, r * 128 : (r + 1) * 128] = block.astype(F32).T.astype(BF)

    await_bytes(gath.at[pl.ds(0, 23)], recv.at[1])

    def spread_three(ref, rows, at, x, keep):
        if keep is not None:
            x = jnp.where(keep, x, 0.0)
        ref[0:rows, pl.ds(at, 128)] = from_left(x).astype(BF)
        ref[rows : 2 * rows, pl.ds(at, 128)] = x.astype(BF)
        ref[2 * rows : 3 * rows, pl.ds(at, 128)] = from_right(x).astype(BF)

    for d in range(6):
        keep = sx > 0 if d < 2 else (sx < 31 if d > 3 else None)
        for h in range(4):
            spread_three(x2s, 64, (d * 6 + h + 1) * 128, gath[d * 4 + h].astype(F32), keep)

    def taps_of(ref, p):
        return jnp.concatenate(
            [ref[:, ((p + kd) * 6 + kh) * 128 : ((p + kd) * 6 + kh + 4) * 128] for kd in range(3) for kh in range(3)],
            axis=0,
        )

    for p in range(4):
        pre = mm(w3[...], taps_of(x2s, p))
        act = smooth_unit(pre)
        keep = sx > 0 if p == 0 else (sx < 31 if p == 3 else None)
        for h in range(4):
            piece = slice(h * 128, (h + 1) * 128)
            if p in (1, 2):
                p3[(p - 1) * 4 + h] = pre[:, piece]
            spread_three(x3s, 128, (p * 6 + h + 1) * 128, act[:, piece].astype(BF).astype(F32), keep)

    grads = []
    for p in range(2):
        pre = mm(w4[...], taps_of(x3s, p))
        here = slice(p * 512, (p + 1) * 512)
        activ[:, here] = smooth_unit(pre).astype(BF)
        grad = (gout[:, here].astype(F32) * smooth_slope(pre) * scale).astype(BF)
        grads.append(grad)
        g4send[p] = grad
    stores = [
        pltpu.make_async_copy(src, dst, load.at[8 + k])
        for k, (src, dst) in enumerate(((activ, activ_out), (all4, out4), (all3, out3), (all2, out2)))
    ]
    push(g4send.at[0], g4halo.at[1], 3, (lax.rem(sx + 31, 32), sy, ch))
    push(g4send.at[1], g4halo.at[0], 3, (lax.rem(sx + 1, 32), sy, ch))
    for kd in range(3):
        for kh in range(3):
            part = None
            for p in range(2):
                at = ((p + kd) * 6 + kh) * 128
                more = mm_nt(grads[p], x3s[:, at : at + 512])
                part = more if part is None else part + more
            for kw in range(3):
                a4[(9 * kd + 3 * kh + kw) // HALF, (9 * kd + 3 * kh + kw) % HALF] = part[:, kw * 128 : (kw + 1) * 128].astype(BF)
    push(a4.at[1 - core], pair4, 16, mate)
    for p in range(2):
        for h in range(4):
            x = grads[p][:, h * 128 : (h + 1) * 128].astype(F32)
            spread_three(g4s, 32, ((p + 1) * 6 + h + 1) * 128, x, None)
    stores[0].start()
    await_bytes(g4halo, recv.at[3])
    for e, p, keep in ((0, 0, sx > 0), (1, 3, sx < 31)):
        for h in range(4):
            x = g4halo[e, :, h * 128 : (h + 1) * 128].astype(F32)
            spread_three(g4s, 32, (p * 6 + h + 1) * 128, x, keep)
    for p in range(2):
        back = mm(wb4[:, :864], taps_of(g4s, p)).astype(BF)
        for h in range(4):
            rs_send[p * 4 + h] = back[:, h * 128 : (h + 1) * 128]

    for group, place in near:
        if place[0] is sx:
            push(rs_send.at[place[2] * 4 + place[1]], rs_recv.at[cell], 4, place)

    def scatter(places, shards, src, dst, mine, slot):
        for other, place in places:
            if shards == 32:
                push(src.at[other], dst.at[mine], slot, place)
            else:
                @pl.when(other < shards)
                def _():
                    push(src.at[other], dst.at[mine], slot, place)

    def spread(places, src, dst, slot):
        for other, place in places:
            push(src, dst, slot, place)

    def total(ref):
        return jnp.sum(ref[...].astype(F32), axis=0)

    await_bytes(pair4, recv.at[16])
    sum4[...] = (a4[core].astype(F32) + pair4[...].astype(F32)).astype(BF)
    scatter(line, HALF, sum4, in4, rank4, 8)
    slope_three = smooth_slope(p3[cell])
    rs_recv[cell] = rs_send[cell]
    await_bytes(rs_recv.at[pl.ds(0, 7)], recv.at[4])
    grad_three = (total(rs_recv) * slope_three).astype(BF)
    g3own[...] = grad_three
    g3buf[5] = grad_three

    for up in (-1, 1, 2, 0):
        d = lax.rem(g - up + 64, 64)
        group, side_ch = lax.div(d, 2), lax.rem(d, 2)
        for side in (2, -1, 1, 0):
            if up or side:
                push(g3own, g3buf.at[(up + 1) * 4 + side + 1], 5, (group, xs[(-side) % 4], side_ch))

    for kd in range(3):
        for kh in range(3):
            at = pl.multiple_of(((ch + 1 + kd) * 6 + sy + kh) * 128, 128)
            part = mm_nt(x2s[:, pl.ds(at, 128)], grad_three).astype(BF)
            for kw in range(3):
                a3[(9 * kd + 3 * kh + kw) // HALF, (9 * kd + 3 * kh + kw) % HALF] = part[kw * 64 : (kw + 1) * 64]
    push(a3.at[1 - core], pair3, 6, mate)

    @pl.when(rank4 < HALF)
    def _():
        in4[rank4] = sum4[rank4]
        await_bytes(in4.at[pl.ds(0, 15)], recv.at[8])
        all4[core, rank4] = total(in4).astype(BF)
        spread(line, all4.at[core, rank4], all4.at[core, rank4], 10)

    await_bytes(pair3, recv.at[6])
    sum3[...] = (a3[core].astype(F32) + pair3[...].astype(F32)).astype(BF)
    scatter(square, HALF, sum3, in3, rank3, 9)

    p1[...] = smooth_slope(p1[...])
    await_bytes(g3buf.at[pl.ds(0, 15)], recv.at[5])

    def spread_grad(d, h):
        keep = (g - 1 + d >= 0) & (g - 1 + d < 64) & (sy - 1 + h >= 0) & (sy - 1 + h < 4)
        spread_three(g3s, 128, (d * 4 + h) * 128, g3buf[d * 4 + h].astype(F32), keep)

    def back_two(a, first, count):
        around = jnp.concatenate(
            [
                g3s[:, ((a + kd) * 4 + kh + first) * 128 : ((a + kd) * 4 + kh + first + count) * 128]
                for kd in range(3)
                for kh in range(3)
            ],
            axis=0,
        )
        back = mm(w3b[...], around)
        for b in range(first, first + count):
            x = back[:, (b - first) * 128 : (b - first + 1) * 128] * s2buf[a * 2 + b]
            if a or b:
                keep = (g + a < 64) & (sy + b < 4)
                x = jnp.where(keep, x, 0.0)
            x = x.astype(BF)
            r = (a * 2 + b) * 128
            g2st[r : r + 64, :] = x
            g2st[r + 64 : r + 128, :] = from_right(x.astype(F32)).astype(BF)

    for d in range(3):
        for h in range(3):
            spread_grad(d, h)
    await_bytes(s2buf.at[pl.ds(0, 3)], recv.at[2])
    back_two(0, 0, 1)
    grad_two = g2st[0:64, :]
    for k in range(7):
        size = 128 if k < 6 else 96
        part = mm_nt(grad_two, a1[k * 128 : k * 128 + size, :]).astype(BF)
        if k == 6:
            part = jnp.concatenate([part, jnp.zeros((64, 32), BF)], axis=1)
        for r in range(4):
            a2[k * 4 + r] = part[r * 16 : (r + 1) * 16]
    scatter(plane, 28, a2, in2, rank, 11)
    for k in range(3):
        spread_grad(k, 3)
    for h in range(4):
        spread_grad(3, h)
    back_two(0, 1, 1)
    back_two(1, 0, 2)
    back_one = mm(wbk[...], g2st[...])
    grad_one = jnp.concatenate(
        [back_one[k * 64 : (k + 1) * 64] * p1[:, k * 128 : (k + 1) * 128] for k in range(4)], axis=1
    ).astype(BF)
    banded = mm_nt(grad_one, vst[:, 256:])
    high = banded.astype(BF)
    rest = (banded - high.astype(F32)).astype(BF)
    local_one = jnp.zeros((32, 128), F32)
    for b in range(2):
        local_one += mm_nt(high[b * 32 : (b + 1) * 32], band[b + 1])
        local_one += mm_nt(rest[b * 32 : (b + 1) * 32], band[b + 1])
    local_one = local_one.astype(BF)
    a2[28] = local_one[:16]
    a2[29] = local_one[16:]
    for shard, row in ((28, 0), (29, 1)):
        @pl.when(rank != shard)
        def _():
            push(a2.at[shard], in2.at[rank], 11, (17 + z * 2, row, 1))
    @pl.when(rank3 < HALF)
    def _():
        in3[rank3] = sum3[rank3]
        await_bytes(in3.at[pl.ds(0, 15)], recv.at[9])
        part3[...] = total(in3).astype(BF)
        mid3[z] = part3[...]
        spread(column, part3, mid3.at[z], 12)

    @pl.when(rank < SMALL)
    def _():
        in2[rank] = a2[rank]
        await_bytes(in2.at[pl.ds(0, 31)], recv.at[11])
        part2[...] = total(in2).astype(BF)
        mid2[z] = part2[...]
        spread(column, part2, mid2.at[z], 13)

    @pl.when(rank3 < HALF)
    def _():
        await_bytes(mid3.at[pl.ds(0, 7)], recv.at[12])
        all3[core, rank3] = total(mid3).astype(BF)
        spread(square, all3.at[core, rank3], all3.at[core, rank3], 14)

    @pl.when(rank < SMALL)
    def _():
        await_bytes(mid2.at[pl.ds(0, 7)], recv.at[13])
        all2[rank] = total(mid2).astype(BF)
        spread(plane, all2.at[rank], all2.at[rank], 15)

    def arrived(me, buf, slot):
        @pl.when(me < HALF)
        def _():
            await_bytes(buf.at[0, pl.ds(0, HALF - 1)], recv.at[slot])

        @pl.when(me >= HALF)
        def _():
            await_bytes(buf.at[0], recv.at[slot])

    arrived(rank4, all4, 10)
    push(all4.at[core], all4.at[core], 17, mate)
    arrived(rank3, all3, 14)
    push(all3.at[core], all3.at[core], 7, mate)
    await_bytes(all4.at[0], recv.at[17])
    stores[1].start()
    await_bytes(all3.at[0], recv.at[7])
    stores[2].start()
    @pl.when(rank < SMALL)
    def _():
        await_bytes(all2.at[pl.ds(0, SMALL - 1)], recv.at[15])

    @pl.when(rank >= SMALL)
    def _():
        await_bytes(all2.at[pl.ds(0, SMALL)], recv.at[15])

    stores[3].start()

    for each in stores:
        each.wait()
    await_bytes(vin, send.at[0])
    await_bytes(gath.at[pl.ds(0, 23)], send.at[1])
    await_bytes(s2buf.at[pl.ds(0, 3)], send.at[2])
    await_bytes(g4send, send.at[3])
    await_bytes(rs_send.at[pl.ds(0, 7)], send.at[4])
    await_bytes(g3buf.at[pl.ds(0, 15)], send.at[5])

    @pl.when(rank < SMALL)
    def _():
        await_bytes(a2.at[pl.ds(0, SMALL - 1)], send.at[11])
        await_bytes(mid2.at[pl.ds(0, 7)], send.at[13])
        await_bytes(in2.at[pl.ds(0, 31)], send.at[15])

    @pl.when(rank >= SMALL)
    def _():
        await_bytes(a2.at[pl.ds(0, SMALL)], send.at[11])

    for pair, total_sum, gathered, slots in ((pair4, sum4, all4, (16, 8, 10, 17)), (pair3, sum3, all3, (6, 9, 14, 7))):
        me = rank4 if pair is pair4 else rank3
        await_bytes(pair, send.at[slots[0]])
        await_bytes(gathered.at[0], send.at[slots[3]])

        @pl.when(me < HALF)
        def _():
            await_bytes(total_sum.at[pl.ds(0, HALF - 1)], send.at[slots[1]])

        @pl.when(me >= HALF)
        def _():
            await_bytes(total_sum, send.at[slots[1]])

    @pl.when(rank4 < HALF)
    def _():
        await_bytes(in4.at[pl.ds(0, 15)], send.at[10])

    @pl.when(rank3 < HALF)
    def _():
        await_bytes(mid3.at[pl.ds(0, 7)], send.at[12])
        await_bytes(in3.at[pl.ds(0, 15)], send.at[14])


def finish_kernel(
    act_in, in2, in3, in4, activ_out, out1, out2, out3, out4,
    act, all2, all3, all4, activ, o1, o2, o3, o4, come, leave,
):
    loads = [
        pltpu.make_async_copy(src, dst, come.at[k])
        for k, (src, dst) in enumerate(((in4, all4), (in3, all3), (act_in, act), (in2, all2)))
    ]
    stores = [
        pltpu.make_async_copy(src, dst, leave.at[k])
        for k, (src, dst) in enumerate(
            ((o4, out4), (o3, out3), (activ, activ_out), (o2, out2), (o1, out1))
        )
    ]
    for each in loads:
        each.start()
    loads[0].wait()
    for t in range(27):
        o4[:, t * 128 : (t + 1) * 128] = all4[t // HALF, t % HALF].astype(F32)
    stores[0].start()
    loads[1].wait()
    for t in range(27):
        o3[t * 64 : (t + 1) * 64, :] = all3[t // HALF, t % HALF].astype(F32)
    stores[1].start()
    loads[2].wait()
    for p in range(2):
        for h in range(4):
            at = (p * 4 + h) * 128
            activ[:, p, h, :] = act[:, at : at + 128]
    stores[2].start()
    loads[3].wait()
    for k in range(7):
        size = 128 if k < 6 else 96
        for r in range(4):
            o2[r * 16 : (r + 1) * 16, k * 128 : k * 128 + size] = all2[k * 4 + r].astype(F32)[:, :size]
    stores[3].start()
    o1[0:16, :] = all2[28].astype(F32)[:, :108]
    o1[16:32, :] = all2[29].astype(F32)[:, :108]
    stores[4].start()
    for each in stores:
        each.wait()


def per_device(volume, w_first, w_second, w_third, w_deep, grad_out):
    cells = 2 * lax.axis_size("sx") * 4 * 128
    scale = 1.0 / float(cells) ** 0.5
    vmem = pl.BlockSpec(memory_space=pltpu.VMEM)

    def kernel(*refs):
        whole_kernel(*refs, scale)

    outs = pl.pallas_call(
        kernel,
        out_shape=(
            jax.ShapeDtypeStruct((32, 1024), BF),
            jax.ShapeDtypeStruct((32, 16, 128), BF),
            jax.ShapeDtypeStruct((2, HALF, 64, 128), BF),
            jax.ShapeDtypeStruct((2, HALF, 32, 128), BF),
        ),
        in_specs=[pl.BlockSpec(memory_space=pltpu.HBM)] * 8,
        out_specs=(pl.BlockSpec(memory_space=pltpu.HBM),) * 4,
        scratch_shapes=[
            pltpu.VMEM((512, 512), BF),
            pltpu.VMEM((96, 288), BF),
            pltpu.VMEM((512, 256), BF),
            pltpu.VMEM((256, 512), BF),
            pltpu.VMEM((896, 128), BF),
            pltpu.VMEM((128, 896), BF),
            pltpu.VMEM((128, 1728), BF),
            pltpu.VMEM((64, 3456), BF),
            pltpu.VMEM((3, 64, 512), BF),
            pltpu.VMEM((288, 768), BF),
            pltpu.VMEM((64, 512), F32),
            pltpu.VMEM((864, 128), BF),
            pltpu.VMEM((24, 64, 128), BF),
            pltpu.VMEM((192, 36 * 128), BF),
            pltpu.VMEM((64, 128), F32),
            pltpu.VMEM((4, 64, 128), F32),
            pltpu.VMEM((8, 128, 128), F32),
            pltpu.VMEM((384, 24 * 128), BF),
            pltpu.VMEM((2, 32, 512), BF),
            pltpu.VMEM((2, 32, 512), BF),
            pltpu.VMEM((96, 24 * 128), BF),
            pltpu.VMEM((8, 128, 128), BF),
            pltpu.VMEM((8, 128, 128), BF),
            pltpu.VMEM((128, 128), BF),
            pltpu.VMEM((16, 128, 128), BF),
            pltpu.VMEM((384, 16 * 128), BF),
            pltpu.VMEM((512, 128), BF),
            pltpu.VMEM((2, HALF, 64, 128), BF),
            pltpu.VMEM((32, 16, 128), BF),
            pltpu.VMEM((2, HALF, 32, 128), BF),
            pltpu.VMEM((HALF, 64, 128), BF),
            pltpu.VMEM((HALF, 32, 128), BF),
            pltpu.VMEM((HALF, 64, 128), BF),
            pltpu.VMEM((HALF, 32, 128), BF),
            pltpu.VMEM((16, 64, 128), BF),
            pltpu.VMEM((32, 16, 128), BF),
            pltpu.VMEM((16, 32, 128), BF),
            pltpu.VMEM((8, 64, 128), BF),
            pltpu.VMEM((8, 16, 128), BF),
            pltpu.VMEM((64, 128), BF),
            pltpu.VMEM((16, 128), BF),
            pltpu.VMEM((2, HALF, 64, 128), BF),
            pltpu.VMEM((32, 16, 128), BF),
            pltpu.VMEM((2, HALF, 32, 128), BF),
            pltpu.VMEM((32, 1024), BF),
            pltpu.VMEM((4, 4, 4, 512), BF),
            pltpu.VMEM((32, 2, 4, 128), BF),
            pltpu.VMEM((64, 512), BF),
            pltpu.VMEM((32, 108), BF),
            pltpu.VMEM((64, 864), BF),
            pltpu.VMEM((1728, 128), BF),
            pltpu.VMEM((32, 3456), BF),
            pltpu.VMEM((32, 1024), BF),
            pltpu.VMEM((224, 256), BF),
            pltpu.VMEM((3, 128, 288), BF),
            pltpu.SemaphoreType.DMA((18,)),
            pltpu.SemaphoreType.DMA((18,)),
            pltpu.SemaphoreType.DMA((12,)),
        ],
        compiler_params=pltpu.CompilerParams(
            collective_id=1, has_side_effects=True, vmem_limit_bytes=60 * 1024 * 1024
        ),
        name="forward_and_backward",
    )(
        volume,
        w_first,
        w_second,
        w_third.T,
        w_deep,
        grad_out,
        jnp.asarray(row_choice(), BF),
        jnp.asarray(band_choice(), BF),
    )
    activ, grad_w1, grad_w2, grad_w3, grad_w4 = pl.pallas_call(
        finish_kernel,
        out_shape=(
            jax.ShapeDtypeStruct((32, 2, 4, 128), BF),
            jax.ShapeDtypeStruct((32, 108), F32),
            jax.ShapeDtypeStruct((64, 864), F32),
            jax.ShapeDtypeStruct((1728, 128), F32),
            jax.ShapeDtypeStruct((32, 3456), F32),
        ),
        in_specs=[pl.BlockSpec(memory_space=pltpu.HBM)] * 4,
        out_specs=(pl.BlockSpec(memory_space=pltpu.HBM),) * 5,
        scratch_shapes=[
            pltpu.VMEM((32, 1024), BF),
            pltpu.VMEM((32, 16, 128), BF),
            pltpu.VMEM((2, HALF, 64, 128), BF),
            pltpu.VMEM((2, HALF, 32, 128), BF),
            pltpu.VMEM((32, 2, 4, 128), BF),
            pltpu.VMEM((32, 108), F32),
            pltpu.VMEM((64, 864), F32),
            pltpu.VMEM((1728, 128), F32),
            pltpu.VMEM((32, 3456), F32),
            pltpu.SemaphoreType.DMA((4,)),
            pltpu.SemaphoreType.DMA((5,)),
        ],
        compiler_params=pltpu.CompilerParams(vmem_limit_bytes=60 * 1024 * 1024),
        name="widen_outputs",
    )(*outs)
    return (activ, grad_w1, grad_w2, grad_w3.T, grad_w4)


def solution(mesh):
    placed = (
        P(None, ("sx", "ch"), "sy", None),
        P(),
        P(),
        P(),
        P(("sy", "ch"), None),
        P(("sy", "ch"), "sx", None, None),
    )
    return jax.shard_map(
        per_device,
        mesh=mesh,
        in_specs=placed,
        out_specs=(P(("sy", "ch"), "sx", None, None), P(), P(), P(), P(("sy", "ch"), None)),
        check_vma=False,
    )
```
